256 devices in a mesh: ta: 128 (over y, x_hi, z, core), lv: 2 (over x_lo).
Axes of the slice: x: 4 (x_hi: 2, x_lo: 2; x = x_hi * 2 + x_lo), y: 4, z: 8, core: 2. Of those that a mesh axis runs over, the one named last changes fastest.
Arguments:
- wind_field: float32 [2, 4096, 31, 360], P('lv', 'ta'), may hold values from -6 to 6
- band_mask: int32 [2, 128, 4096], P(None, 'ta'), may hold values from 0 to 1, as said below
- sym_flag: int32 [16], replicated, may hold values from 0 to 1
Outputs:
- kelvin_wind: float32 [2, 4096, 31, 360], P('lv', 'ta')
- mjo_wind: float32 [2, 4096, 31, 360], P('lv', 'ta')
- shear_mjo: float32 [4096, 31, 360], P(('ta', 'lv'))
The draws below stay inside these ranges and needn't reach their ends.
Inputs may be any that keep to these rules, and one draw needn't show every extreme that they name: `band_mask`: for each band and wavenumber, the entries equal to 1 form one run of consecutive frequency indices holding at least one entry and not wrapping past index 4095.
All inputs are finite; a program needn't handle non-finite values.
Results may differ from the reference program's by a relative error of at most 0.0001.
Values sent between devices are 32-bit elements; how exact they have to be, the bound alone decides.
No kernel may reach another device: no remote copies, remote signals or barrier semaphores. Data moves between devices by JAX's collectives and lax.ppermute only.
A program may use at most 64 MiB of HBM per device.

```python
import jax
import jax.numpy as jnp

NLON = 360
NLAT = 31
KM = 128
NT = 4096
NPAIR = 16
LV = 2


def draw_band_mask(key, part):
    key = jax.random.fold_in(key, 7)
    first_key, second_key = jax.random.split(key)
    start_index = jax.random.randint(first_key, (2, KM, 1), 0, NT // 2)
    run_length = jax.random.randint(second_key, (2, KM, 1), 1, NT // 2 + 1)
    frequency = jnp.arange(NT, dtype=jnp.int32)[None, None, :]
    inside = (frequency >= start_index) & (frequency < start_index + run_length)
    return jnp.where(inside, 1, 0).astype(jnp.int32)


def set_ends(drawn, rng, smallest, largest):
    longest = drawn.shape.index(max(drawn.shape))
    spots = []
    for shift in (0, 1):
        where = [jax.random.randint(jax.random.fold_in(rng, axis), (), 0, length) for axis, length in enumerate(drawn.shape)]
        where[longest] = (where[longest] + shift) % drawn.shape[longest]
        spots.append(tuple(where))
    return drawn.at[spots[0]].set(smallest).at[spots[1]].set(largest)


def levels(key, shape, shards, smallest, largest):
    level = 1.0
    for axis_at, shards_of in shards:
        steps = jax.random.uniform(jax.random.fold_in(jax.random.fold_in(key, 6), axis_at), (shards_of,), jnp.float32, smallest / len(shards), largest / len(shards))
        level = level * jnp.repeat(jnp.exp(steps), shape[axis_at] // shards_of).reshape((-1,) + (1,) * (len(shape) - 1 - axis_at))
    return level


def bell_draw(key, extent, width, limit, shards=(), held_as=jnp.bfloat16):
    loudness = levels(key, extent, shards, -0.22, 0.18) if shards else 1.0
    drawn = jax.random.normal(key, extent, jnp.float32) * width * loudness
    return jnp.minimum(jnp.maximum(drawn, -limit), limit).astype(held_as)


def setup_inputs(seed: int = 0) -> dict:
    keys = jax.random.split(jax.random.key(seed), 4)
    return {
        "wind_field": bell_draw(keys[0], (LV, NT, NLAT, NLON), 1.0, 6.0, ((0, 2), (1, 128)), jnp.float32),
        "band_mask": draw_band_mask(jax.random.fold_in(keys[3], 71), 0),
        "sym_flag": set_ends(jax.random.randint(keys[2], (NPAIR,), 0, 2), jax.random.fold_in(keys[2], 1), 0, 1).astype(jnp.int32),
    }


def reference(wind_field, band_mask, sym_flag):
    centre = NPAIR - 1
    sign_row = 1.0 - 2.0 * sym_flag.astype(jnp.float32)
    weight = band_mask.astype(jnp.float32)
    kelvin_levels = []
    mjo_levels = []
    for level_index in range(LV):
        northern = wind_field[level_index, :, centre:, :]
        southern = wind_field[level_index, :, centre::-1, :]
        component = jnp.where(sym_flag[None, :, None] == 1, 0.5 * (northern - southern), 0.5 * (northern + southern))
        zonal_coef = jnp.fft.rfft(component, axis=-1)[:, :, :KM] / NLON
        spectrum = jnp.fft.fft(zonal_coef, axis=0)
        banded = []
        for band_index in range(2):
            series = jnp.fft.ifft(spectrum * weight[band_index].T[:, None, :], axis=0)
            padded = jnp.pad(series, ((0, 0), (0, 0), (0, NLON // 2 + 1 - KM))) * NLON
            waves = jnp.fft.irfft(padded, n=NLON, axis=-1)
            mirrored = (sign_row[None, :, None] * waves)[:, :0:-1, :]
            banded.append(jnp.concatenate([mirrored, waves], axis=1).astype(jnp.float32))
        kelvin_levels.append(banded[0])
        mjo_levels.append(banded[1])
    kelvin_wind = jnp.stack(kelvin_levels)
    mjo_wind = jnp.stack(mjo_levels)
    shear_mjo = mjo_wind[1] - mjo_wind[0]
    return kelvin_wind, mjo_wind, shear_mjo
```

```python
import functools

import jax
import jax.numpy as jnp
import ml_dtypes
import numpy as np
from jax import lax
from jax.experimental import pallas as pl
from jax.experimental.pallas import tpu as pltpu
from jax.sharding import PartitionSpec as P

NLON = 360
NLAT = 31
KM = 128
NT = 4096
NPAIR = 16
BLOCK = 32
HALF = 16
CENTRE = NPAIR - 1
F32 = jnp.float32
BF16 = jnp.bfloat16


def halves(table):
    table = np.asarray(table, np.float32)
    high = table.astype(ml_dtypes.bfloat16)
    low = (table - high.astype(np.float32)).astype(ml_dtypes.bfloat16)
    return np.stack([high, low])


def turn(rows, cols, length):
    angle = 2.0 * np.pi / length * (np.outer(rows, cols) % length)
    return np.cos(angle), np.sin(angle)


def zonal_forward_table():
    cosine, sine = turn(np.arange(KM), np.arange(NLON), NLON)
    return halves(np.concatenate([cosine, -sine]) / NLON)


def zonal_inverse_table():
    cosine, sine = turn(np.arange(KM), np.arange(NLON), NLON)
    doubled = np.where(np.arange(KM) == 0, 1.0, 2.0)[:, None]
    return halves(np.concatenate([cosine * doubled, -sine * doubled]))


def outer_tables():
    cosine, sine = turn(np.arange(128), np.arange(128), 128)
    forward = np.block([[cosine, sine], [-sine, cosine]])
    inverse = np.block([[cosine, -sine], [sine, cosine]]) / NT
    return halves(forward), halves(inverse)


def inner_tables():
    cosine, sine = turn(np.arange(BLOCK), np.arange(BLOCK), BLOCK)
    eye = np.eye(4)
    cos4, sin4 = np.kron(eye, cosine), np.kron(eye, sine)
    forward = np.block([[cos4, -sin4], [sin4, cos4]])
    order = np.arange(128).reshape(4, 2, HALF).transpose(1, 0, 2).reshape(-1)
    cos4, sin4 = cos4[:, order], sin4[:, order]
    inverse = np.block([[cos4, sin4], [-sin4, cos4]])
    return halves(forward), halves(inverse)


def twist_tables():
    time = np.tile(np.arange(BLOCK), 4)
    order = np.arange(128).reshape(4, 2, HALF).transpose(1, 0, 2).reshape(-1)
    cosine, sine = turn(np.arange(128), time, NT)
    forward = np.stack([cosine, -sine])
    inverse = np.stack([cosine[:, order], sine[:, order]])
    return np.concatenate([forward, inverse]).astype(np.float32)


def split(value):
    high = value.astype(BF16)
    return high, (value - high.astype(F32)).astype(BF16)


def product(left, right, contract):
    dims = (contract, ((), ()))

    def dot(a, b):
        return lax.dot_general(a, b, dims, preferred_element_type=F32)

    return dot(left[0], right[0]) + (dot(left[0], right[1]) + dot(left[1], right[0]))


ROWS_COLS = ((1,), (0,))
ROWS_ROWS = ((1,), (1,))
COLS_COLS = ((0,), (0,))


def zonal_kernel(sym_ref, wind_ref, table_ref, out_ref):
    parts = []
    for j in range(NPAIR):
        sign = 1.0 - 2.0 * sym_ref[j].astype(F32)
        parts.append(0.5 * (wind_ref[CENTRE + j] + sign * wind_ref[CENTRE - j]))
    component = split(jnp.concatenate(parts, axis=0))
    coef = product((table_ref[0], table_ref[1]), component, ROWS_ROWS)
    for c in range(2):
        for jq in range(4):
            tile = coef[c * 128 : (c + 1) * 128, jq * 128 : (jq + 1) * 128]
            out_ref[pl.ds(c * 4 + jq, 128, stride=8), :] = tile


def time_kernel(
    series_ref, mask_ref, spread_ref, outer_f, inner_f, inner_i, outer_i, twist_ref, out_ref
):
    def rows(ref):
        return ref[0], ref[1]

    def wide(c):
        return jnp.concatenate(
            [series_ref[pl.ds(c * 4 + jq, 128, stride=8), :] for jq in range(4)], axis=1
        )

    operand = split(jnp.concatenate([wide(0), wide(1)], axis=0))
    partial = product(rows(outer_f), operand, ROWS_COLS)
    twisted = []
    for jq in range(4):
        lanes = slice(jq * 128, (jq + 1) * 128)
        real, imag = partial[:128, lanes], partial[128:, lanes]
        twisted.append(
            jnp.concatenate(
                [
                    real * twist_ref[0] - imag * twist_ref[1],
                    real * twist_ref[1] + imag * twist_ref[0],
                ],
                axis=1,
            )
        )
    spectrum = product(split(jnp.concatenate(twisted, axis=0)), rows(inner_f), ROWS_COLS)
    low_lanes = lax.broadcasted_iota(jnp.int32, (128, 128), 1) < 64
    for b in range(2):
        keep = lax.dot_general(
            mask_ref[b].astype(F32).astype(BF16),
            spread_ref[...],
            (COLS_COLS, ((), ())),
            preferred_element_type=F32,
        )
        keep = jnp.concatenate([jnp.concatenate([keep, keep], axis=1)] * 4, axis=0)
        unwound = product(split(spectrum * keep), rows(inner_i), ROWS_COLS)
        real_tiles, imag_tiles = [], []
        for jq in range(4):
            real = unwound[jq * 128 : (jq + 1) * 128, :128]
            imag = unwound[jq * 128 : (jq + 1) * 128, 128:]
            real_tiles.append(real * twist_ref[2] - imag * twist_ref[3])
            imag_tiles.append(real * twist_ref[3] + imag * twist_ref[2])

        def regroup(tiles):
            first = [
                jnp.where(low_lanes, tiles[2 * jh], pltpu.roll(tiles[2 * jh + 1], 64, 1))
                for jh in range(2)
            ]
            second = [
                jnp.where(low_lanes, pltpu.roll(tiles[2 * jh], 64, 1), tiles[2 * jh + 1])
                for jh in range(2)
            ]
            return jnp.concatenate(first + second, axis=1)

        stacked = jnp.concatenate([regroup(real_tiles), regroup(imag_tiles)], axis=0)
        restored = product(rows(outer_i), split(stacked), ROWS_COLS)
        for th in range(2):
            for c in range(2):
                for jh in range(2):
                    row = ((b * 2 + th) * 2 + c) * 2 + jh
                    lanes = slice((th * 2 + jh) * 128, (th * 2 + jh + 1) * 128)
                    out_ref[pl.ds(row, 128, stride=16), :] = restored[c * 128 : (c + 1) * 128, lanes]


def write_rows(out_ref, waves, sym_ref):
    for j in range(NPAIR):
        block = waves[j * HALF : (j + 1) * HALF, :]
        out_ref[CENTRE + j] = block
        if j:
            sign = 1.0 - 2.0 * sym_ref[j].astype(F32)
            out_ref[CENTRE - j] = sign * block


def waves_kernel(sym_ref, coef_ref, table_ref, kelvin_ref, mjo_ref):
    th = pl.program_id(0)
    table = (table_ref[0], table_ref[1])
    for b, out_ref in ((0, kelvin_ref), (1, mjo_ref)):
        row = (b * 2 + th) * 4
        coef = jnp.concatenate(
            [
                jnp.concatenate(
                    [coef_ref[pl.ds(row + c * 2 + jh, 128, stride=16), :] for jh in range(2)],
                    axis=1,
                )
                for c in range(2)
            ],
            axis=0,
        )
        write_rows(out_ref, product(split(coef), table, COLS_COLS), sym_ref)


def pick_kernel(level_ref, coef_ref, own_ref, other_ref):
    level = level_ref[0]
    for out_ref, th in ((own_ref, level), (other_ref, 1 - level)):
        for r in range(4):
            out_ref[pl.ds(r * 128, 128), :] = coef_ref[pl.ds(8 + th * 4 + r, 128, stride=16), :]


def shear_kernel(level_ref, sym_ref, own_ref, partner_ref, table_ref, out_ref):
    sign = 2.0 * level_ref[0].astype(F32) - 1.0
    apart = sign * (own_ref[...] - partner_ref[...])
    coef = jnp.concatenate(
        [
            jnp.concatenate([apart[c * 256 : c * 256 + 128], apart[c * 256 + 128 : c * 256 + 256]], axis=1)
            for c in range(2)
        ],
        axis=0,
    )
    waves = product(split(coef), (table_ref[0], table_ref[1]), COLS_COLS)
    write_rows(out_ref, waves, sym_ref)


SMEM = pl.BlockSpec(memory_space=pltpu.SMEM)
VMEM = pl.BlockSpec(memory_space=pltpu.VMEM)


def call(kernel, in_specs, out_shapes, macs, moved, **kwargs):
    return pl.pallas_call(
        kernel,
        in_specs=in_specs,
        out_shape=out_shapes,
        cost_estimate=pl.CostEstimate(flops=2 * macs, bytes_accessed=moved, transcendentals=0),
        compiler_params=pltpu.CompilerParams(vmem_limit_bytes=32 << 20),
        **kwargs,
    )


def shape(*sizes):
    return jax.ShapeDtypeStruct(sizes, F32)


def body(wind_field, band_mask, sym_flag):
    level = lax.axis_index("lv").astype(jnp.int32).reshape(1)
    record = jnp.transpose(wind_field[0], (1, 0, 2))
    outer_f, outer_i = outer_tables()
    inner_f, inner_i = inner_tables()
    spread = np.tile(np.eye(BLOCK), (1, 4)).astype(ml_dtypes.bfloat16)
    inverse_table = zonal_inverse_table()

    coef = call(zonal_kernel, [SMEM, VMEM, VMEM], shape(1024, 128), 3 * 512 * 360 * 256, 3 << 20, out_specs=VMEM)(
        sym_flag, record, zonal_forward_table()
    )
    series = lax.all_to_all(coef, "ta", split_axis=0, concat_axis=0, tiled=True)
    filtered = call(
        time_kernel, [VMEM] * 8, shape(2048, 128), 3 * 4 * 512 * 256 * 256, 4 << 20, out_specs=VMEM
    )(
        series,
        band_mask.reshape(2, BLOCK, 128),
        spread,
        outer_f,
        inner_f,
        inner_i,
        outer_i,
        twist_tables(),
    )
    returned = lax.all_to_all(filtered, "ta", split_axis=0, concat_axis=0, tiled=True)
    own, other = call(
        pick_kernel, [SMEM, VMEM], (shape(512, 128), shape(512, 128)), 1 << 10, 1 << 20, out_specs=(VMEM, VMEM)
    )(level, returned)
    partner = lax.ppermute(other, "lv", [(0, 1), (1, 0)])
    block = pl.BlockSpec((NLAT, HALF, NLON), lambda i: (0, i, 0))
    kelvin, mjo = call(
        waves_kernel,
        [SMEM, VMEM, VMEM],
        (shape(NLAT, BLOCK, NLON), shape(NLAT, BLOCK, NLON)),
        3 * 1024 * 360 * 256,
        5 << 20,
        grid=(2,),
        out_specs=(block, block),
    )(sym_flag, returned, inverse_table)
    shear = call(
        shear_kernel, [SMEM, SMEM, VMEM, VMEM, VMEM], shape(NLAT, HALF, NLON), 3 * 256 * 360 * 256, 2 << 20, out_specs=VMEM
    )(level, sym_flag, own, partner, inverse_table)
    return (
        jnp.transpose(kelvin, (1, 0, 2))[None],
        jnp.transpose(mjo, (1, 0, 2))[None],
        jnp.transpose(shear, (1, 0, 2)),
    )


def solution(mesh):
    placed = (P("lv", "ta", None, None), P(None, "ta", None), P())
    return jax.shard_map(
        body,
        mesh=mesh,
        in_specs=placed,
        out_specs=(
            P("lv", "ta", None, None),
            P("lv", "ta", None, None),
            P(("ta", "lv"), None, None),
        ),
        check_vma=False,
    )
```

```python
import jax
import jax.numpy as jnp
import ml_dtypes
import numpy as np
from jax import lax
from jax.experimental import pallas as pl
from jax.experimental.pallas import tpu as pltpu
from jax.sharding import PartitionSpec as P

NLON = 360
NLAT = 31
KM = 128
NT = 4096
NPAIR = 16
BLOCK = 32
HALF = 16
CENTRE = NPAIR - 1
SHIFT = (2, 1, 4, 0)
F32 = jnp.float32
BF16 = jnp.bfloat16


def member_order():
    index = np.arange(128).reshape(4, 2, 8, 2)
    return np.roll(index, SHIFT, axis=(0, 1, 2, 3)).reshape(-1)


def exchange(blocks):
    groups = [[int(member) for member in member_order()]]
    return lax.all_to_all(
        blocks, "ta", split_axis=0, concat_axis=0, axis_index_groups=groups, tiled=True
    )


def halves(table):
    table = np.asarray(table, np.float32)
    high = table.astype(ml_dtypes.bfloat16)
    low = (table - high.astype(np.float32)).astype(ml_dtypes.bfloat16)
    return np.stack([high, low])


def turn(rows, cols, length):
    angle = 2.0 * np.pi / length * (np.outer(rows, cols) % length)
    return np.cos(angle), np.sin(angle)


def zonal_forward_table():
    cosine, sine = turn(member_order(), np.arange(NLON), NLON)
    return halves(np.concatenate([cosine, -sine]) / NLON)


def zonal_inverse_table():
    cosine, sine = turn(member_order(), np.arange(NLON), NLON)
    doubled = np.where(member_order() == 0, 1.0, 2.0)[:, None]
    return halves(np.concatenate([cosine * doubled, -sine * doubled]))


def outer_tables():
    cosine, sine = turn(np.arange(128), member_order(), 128)
    forward = np.block([[cosine, sine], [-sine, cosine]])
    inverse = np.block([[cosine.T, -sine.T], [sine.T, cosine.T]]) / NT
    return halves(forward), halves(inverse)


def inner_tables():
    cosine, sine = turn(np.arange(BLOCK), np.arange(BLOCK), BLOCK)
    eye = np.eye(4)
    cos4, sin4 = np.kron(eye, cosine), np.kron(eye, sine)
    forward = np.block([[cos4, -sin4], [sin4, cos4]])
    order = np.arange(128).reshape(4, 2, HALF).transpose(1, 0, 2).reshape(-1)
    cos4, sin4 = cos4[:, order], sin4[:, order]
    inverse = np.block([[cos4, sin4], [-sin4, cos4]])
    return halves(forward), halves(inverse)


def twist_tables():
    time = np.tile(np.arange(BLOCK), 4)
    order = np.arange(128).reshape(4, 2, HALF).transpose(1, 0, 2).reshape(-1)
    cosine, sine = turn(np.arange(128), time, NT)
    forward = np.stack([cosine, -sine])
    inverse = np.stack([cosine[:, order], sine[:, order]])
    return np.concatenate([forward, inverse]).astype(np.float32)


def split(value):
    high = value.astype(BF16)
    return high, (value - high.astype(F32)).astype(BF16)


def product(left, right, contract):
    dims = (contract, ((), ()))

    def dot(a, b):
        return lax.dot_general(a, b, dims, preferred_element_type=F32)

    return dot(left[0], right[0]) + (dot(left[0], right[1]) + dot(left[1], right[0]))


ROWS_COLS = ((1,), (0,))
ROWS_ROWS = ((1,), (1,))
COLS_COLS = ((0,), (0,))


def zonal_kernel(
    sym_hbm, wind_hbm, table_hbm, out_ref, sym_ref, wind_ref, table_ref, arrived
):
    loads = [
        pltpu.make_async_copy(source, target, arrived.at[i])
        for i, (source, target) in enumerate(
            ((sym_hbm, sym_ref), (wind_hbm, wind_ref), (table_hbm, table_ref))
        )
    ]
    for load in loads:
        load.start()
    for load in loads:
        load.wait()
    parts = []
    for j in range(NPAIR):
        sign = 1.0 - 2.0 * sym_ref[j].astype(F32)
        parts.append(0.5 * (wind_ref[CENTRE + j] + sign * wind_ref[CENTRE - j]))
    component = split(jnp.concatenate(parts, axis=0))
    coef = product((table_ref[0], table_ref[1]), component, ROWS_ROWS)
    for c in range(2):
        for jq in range(4):
            tile = coef[c * 128 : (c + 1) * 128, jq * 128 : (jq + 1) * 128]
            out_ref[pl.ds(c * 4 + jq, 128, stride=8), :] = tile


def time_kernel(
    series_ref, mask_ref, spread_ref, outer_f, inner_f, inner_i, outer_i, twist_ref, out_ref
):
    def rows(ref):
        return ref[0], ref[1]

    def wide(c):
        return jnp.concatenate(
            [series_ref[pl.ds(c * 4 + jq, 128, stride=8), :] for jq in range(4)], axis=1
        )

    operand = split(jnp.concatenate([wide(0), wide(1)], axis=0))
    partial = product(rows(outer_f), operand, ROWS_COLS)
    twisted = []
    for jq in range(4):
        lanes = slice(jq * 128, (jq + 1) * 128)
        real, imag = partial[:128, lanes], partial[128:, lanes]
        twisted.append(
            jnp.concatenate(
                [
                    real * twist_ref[0] - imag * twist_ref[1],
                    real * twist_ref[1] + imag * twist_ref[0],
                ],
                axis=1,
            )
        )
    spectrum = product(split(jnp.concatenate(twisted, axis=0)), rows(inner_f), ROWS_COLS)
    low_lanes = lax.broadcasted_iota(jnp.int32, (128, 128), 1) < 64
    for b in range(2):
        keep = lax.dot_general(
            mask_ref[b].astype(F32).astype(BF16),
            spread_ref[...],
            (COLS_COLS, ((), ())),
            preferred_element_type=F32,
        )
        keep = jnp.concatenate([jnp.concatenate([keep, keep], axis=1)] * 4, axis=0)
        unwound = product(split(spectrum * keep), rows(inner_i), ROWS_COLS)
        real_tiles, imag_tiles = [], []
        for jq in range(4):
            real = unwound[jq * 128 : (jq + 1) * 128, :128]
            imag = unwound[jq * 128 : (jq + 1) * 128, 128:]
            real_tiles.append(real * twist_ref[2] - imag * twist_ref[3])
            imag_tiles.append(real * twist_ref[3] + imag * twist_ref[2])

        def regroup(tiles):
            first = [
                jnp.where(low_lanes, tiles[2 * jh], pltpu.roll(tiles[2 * jh + 1], 64, 1))
                for jh in range(2)
            ]
            second = [
                jnp.where(low_lanes, pltpu.roll(tiles[2 * jh], 64, 1), tiles[2 * jh + 1])
                for jh in range(2)
            ]
            return jnp.concatenate(first + second, axis=1)

        stacked = jnp.concatenate([regroup(real_tiles), regroup(imag_tiles)], axis=0)
        restored = product(rows(outer_i), split(stacked), ROWS_COLS)
        for th in range(2):
            for c in range(2):
                for jh in range(2):
                    row = ((b * 2 + th) * 2 + c) * 2 + jh
                    lanes = slice((th * 2 + jh) * 128, (th * 2 + jh + 1) * 128)
                    out_ref[pl.ds(row, 128, stride=16), :] = restored[c * 128 : (c + 1) * 128, lanes]


def write_rows(out_ref, waves, sym_ref):
    for j in range(NPAIR):
        block = waves[j * HALF : (j + 1) * HALF, :]
        out_ref[CENTRE + j] = block
        if j:
            sign = 1.0 - 2.0 * sym_ref[j].astype(F32)
            out_ref[CENTRE - j] = sign * block


def waves_kernel(sym_ref, coef_ref, table_ref, kelvin_ref, mjo_ref):
    th = pl.program_id(0)
    table = (table_ref[0], table_ref[1])
    for b, out_ref in ((0, kelvin_ref), (1, mjo_ref)):
        row = (b * 2 + th) * 4
        coef = jnp.concatenate(
            [
                jnp.concatenate(
                    [coef_ref[pl.ds(row + c * 2 + jh, 128, stride=16), :] for jh in range(2)],
                    axis=1,
                )
                for c in range(2)
            ],
            axis=0,
        )
        write_rows(out_ref, product(split(coef), table, COLS_COLS), sym_ref)


def pick_kernel(level_ref, coef_ref, own_ref, other_ref):
    level = level_ref[0]
    for out_ref, th in ((own_ref, level), (other_ref, 1 - level)):
        for r in range(4):
            out_ref[pl.ds(r * 128, 128), :] = coef_ref[pl.ds(8 + th * 4 + r, 128, stride=16), :]


def shear_kernel(level_ref, sym_ref, own_ref, partner_ref, table_ref, out_ref):
    sign = 2.0 * level_ref[0].astype(F32) - 1.0
    apart = sign * (own_ref[...] - partner_ref[...])
    coef = jnp.concatenate(
        [
            jnp.concatenate([apart[c * 256 : c * 256 + 128], apart[c * 256 + 128 : c * 256 + 256]], axis=1)
            for c in range(2)
        ],
        axis=0,
    )
    waves = product(split(coef), (table_ref[0], table_ref[1]), COLS_COLS)
    write_rows(out_ref, waves, sym_ref)


SMEM = pl.BlockSpec(memory_space=pltpu.SMEM)
VMEM = pl.BlockSpec(memory_space=pltpu.VMEM)
HBM = pl.BlockSpec(memory_space=pltpu.HBM)


def call(kernel, in_specs, out_shapes, macs, moved, **kwargs):
    return pl.pallas_call(
        kernel,
        in_specs=in_specs,
        out_shape=out_shapes,
        cost_estimate=pl.CostEstimate(flops=2 * macs, bytes_accessed=moved, transcendentals=0),
        compiler_params=pltpu.CompilerParams(vmem_limit_bytes=32 << 20),
        **kwargs,
    )


def in_hbm(array):
    return pltpu.with_memory_space_constraint(array, pltpu.HBM)


def shape(*sizes):
    return jax.ShapeDtypeStruct(sizes, F32)


def body(wind_field, band_mask, sym_flag):
    level = lax.axis_index("lv").astype(jnp.int32).reshape(1)
    record = jnp.transpose(wind_field[0], (1, 0, 2))
    outer_f, outer_i = outer_tables()
    inner_f, inner_i = inner_tables()
    spread = np.tile(np.eye(BLOCK), (1, 4)).astype(ml_dtypes.bfloat16)
    inverse_table = zonal_inverse_table()

    coef = call(
        zonal_kernel,
        [HBM] * 3,
        shape(1024, 128),
        3 * 512 * 360 * 256,
        3 << 20,
        out_specs=VMEM,
        scratch_shapes=[
            pltpu.SMEM((NPAIR,), jnp.int32),
            pltpu.VMEM((NLAT, BLOCK, NLON), F32),
            pltpu.VMEM((2, 2 * KM, NLON), BF16),
            pltpu.SemaphoreType.DMA((3,)),
        ],
    )(in_hbm(sym_flag), in_hbm(record), in_hbm(jnp.asarray(zonal_forward_table())))
    series = exchange(coef)
    filtered = call(
        time_kernel, [VMEM] * 8, shape(2048, 128), 3 * 4 * 512 * 256 * 256, 4 << 20, out_specs=VMEM
    )(
        series,
        band_mask.reshape(2, BLOCK, 128),
        spread,
        outer_f,
        inner_f,
        inner_i,
        outer_i,
        twist_tables(),
    )
    returned = exchange(filtered)
    own, other = call(
        pick_kernel, [SMEM, VMEM], (shape(512, 128), shape(512, 128)), 1 << 10, 1 << 20, out_specs=(VMEM, VMEM)
    )(level, returned)
    partner = lax.ppermute(other, "lv", [(0, 1), (1, 0)])
    block = pl.BlockSpec((NLAT, HALF, NLON), lambda i: (0, i, 0))
    kelvin, mjo = call(
        waves_kernel,
        [SMEM, VMEM, VMEM],
        (shape(NLAT, BLOCK, NLON), shape(NLAT, BLOCK, NLON)),
        3 * 1024 * 360 * 256,
        5 << 20,
        grid=(2,),
        out_specs=(block, block),
    )(sym_flag, returned, inverse_table)
    shear = call(
        shear_kernel, [SMEM, SMEM, VMEM, VMEM, VMEM], shape(NLAT, HALF, NLON), 3 * 256 * 360 * 256, 2 << 20, out_specs=VMEM
    )(level, sym_flag, own, partner, inverse_table)
    return (
        jnp.transpose(kelvin, (1, 0, 2))[None],
        jnp.transpose(mjo, (1, 0, 2))[None],
        jnp.transpose(shear, (1, 0, 2)),
    )


def solution(mesh):
    placed = (P("lv", "ta", None, None), P(None, "ta", None), P())
    return jax.shard_map(
        body,
        mesh=mesh,
        in_specs=placed,
        out_specs=(
            P("lv", "ta", None, None),
            P("lv", "ta", None, None),
            P(("ta", "lv"), None, None),
        ),
        check_vma=False,
    )
```

```python
import jax
import jax.numpy as jnp
import ml_dtypes
import numpy as np
from jax import lax
from jax.experimental import pallas as pl
from jax.experimental.pallas import tpu as pltpu
from jax.sharding import PartitionSpec as P

NLON = 360
NLAT = 31
KM = 128
NT = 4096
NPAIR = 16
BLOCK = 32
HALF = 16
CENTRE = NPAIR - 1
SHIFT = (2, 1, 4, 0)
F32 = jnp.float32
BF16 = jnp.bfloat16


def member_order():
    index = np.arange(128).reshape(4, 2, 8, 2)
    return np.roll(index, SHIFT, axis=(0, 1, 2, 3)).reshape(-1)


def exchange(blocks):
    groups = [[int(member) for member in member_order()]]
    return lax.all_to_all(
        blocks, "ta", split_axis=0, concat_axis=0, axis_index_groups=groups, tiled=True
    )


def halves(table):
    table = np.asarray(table, np.float32)
    high = table.astype(ml_dtypes.bfloat16)
    low = (table - high.astype(np.float32)).astype(ml_dtypes.bfloat16)
    return np.stack([high, low])


def turn(rows, cols, length):
    angle = 2.0 * np.pi / length * (np.outer(rows, cols) % length)
    return np.cos(angle), np.sin(angle)


def zonal_forward_table():
    cosine, sine = turn(member_order(), np.arange(NLON), NLON)
    return halves(np.concatenate([cosine, -sine]) / NLON)


def zonal_inverse_table():
    cosine, sine = turn(member_order(), np.arange(NLON), NLON)
    doubled = np.where(member_order() == 0, 1.0, 2.0)[:, None]
    return halves(np.concatenate([cosine * doubled, -sine * doubled]))


def outer_tables():
    cosine, sine = turn(np.arange(128), member_order(), 128)
    forward = np.block([[cosine, sine], [-sine, cosine]])
    inverse = np.block([[cosine.T, -sine.T], [sine.T, cosine.T]]) / NT
    return halves(forward), halves(inverse)


def inner_tables():
    cosine, sine = turn(np.arange(BLOCK), np.arange(BLOCK), BLOCK)
    eye = np.eye(4)
    cos4, sin4 = np.kron(eye, cosine), np.kron(eye, sine)
    forward = np.block([[cos4, -sin4], [sin4, cos4]])
    order = np.arange(128).reshape(4, 2, HALF).transpose(1, 0, 2).reshape(-1)
    cos4, sin4 = cos4[:, order], sin4[:, order]
    inverse = np.block([[cos4, sin4], [-sin4, cos4]])
    return halves(forward), halves(inverse)


def twist_tables():
    time = np.tile(np.arange(BLOCK), 4)
    order = np.arange(128).reshape(4, 2, HALF).transpose(1, 0, 2).reshape(-1)
    cosine, sine = turn(np.arange(128), time, NT)
    forward = np.stack([cosine, -sine])
    inverse = np.stack([cosine[:, order], sine[:, order]])
    return np.concatenate([forward, inverse]).astype(np.float32)


def split(value):
    high = value.astype(BF16)
    return high, (value - high.astype(F32)).astype(BF16)


def product(left, right, contract):
    dims = (contract, ((), ()))

    def dot(a, b):
        return lax.dot_general(a, b, dims, preferred_element_type=F32)

    return dot(left[0], right[0]) + (dot(left[0], right[1]) + dot(left[1], right[0]))


ROWS_COLS = ((1,), (0,))
ROWS_ROWS = ((1,), (1,))
COLS_COLS = ((0,), (0,))


def zonal_kernel(
    sym_hbm, wind_hbm, table_hbm, out_ref, sign_ref, sym_ref, wind_ref, table_ref, arrived
):
    loads = [
        pltpu.make_async_copy(source, target, arrived.at[i])
        for i, (source, target) in enumerate(
            ((sym_hbm, sym_ref), (wind_hbm, wind_ref), (table_hbm, table_ref))
        )
    ]
    for load in loads:
        load.start()
    for load in loads:
        load.wait()
    parts = []
    for j in range(NPAIR):
        sign = 1.0 - 2.0 * sym_ref[j].astype(F32)
        sign_ref[pl.ds(j, 1), :] = jnp.full((1, NLON), sign, F32)
        parts.append(0.5 * (wind_ref[CENTRE + j] + sign * wind_ref[CENTRE - j]))
    component = split(jnp.concatenate(parts, axis=0))
    coef = product((table_ref[0], table_ref[1]), component, ROWS_ROWS)
    for c in range(2):
        for jq in range(4):
            tile = coef[c * 128 : (c + 1) * 128, jq * 128 : (jq + 1) * 128]
            out_ref[pl.ds(c * 4 + jq, 128, stride=8), :] = tile


def time_kernel(
    series_ref, mask_ref, spread_ref, outer_f, inner_f, inner_i, outer_i, twist_ref, out_ref
):
    def rows(ref):
        return ref[0], ref[1]

    def tile(value, c, q):
        return value[c * 128 : (c + 1) * 128, q * 128 : (q + 1) * 128]

    def square(tiles):
        return jnp.concatenate([jnp.concatenate(row, axis=1) for row in tiles], axis=0)

    def partial_dft(jh):
        blocks = [
            [series_ref[pl.ds(c * 4 + jh * 2 + q, 128, stride=8), :] for q in range(2)]
            for c in range(2)
        ]
        return product(rows(outer_f), split(square(blocks)), ROWS_COLS)

    def twist(value):
        turned = []
        for q in range(2):
            real, imag = tile(value, 0, q), tile(value, 1, q)
            turned.append(
                [
                    real * twist_ref[0] - imag * twist_ref[1],
                    real * twist_ref[1] + imag * twist_ref[0],
                ]
            )
        return square(turned)

    low_lanes = lax.broadcasted_iota(jnp.int32, (128, 128), 1) < 64

    def untwist(value):
        turned = [[], []]
        for q in range(2):
            real, imag = tile(value, q, 0), tile(value, q, 1)
            turned[0].append(real * twist_ref[2] - imag * twist_ref[3])
            turned[1].append(real * twist_ref[3] + imag * twist_ref[2])
        return square(
            [
                [
                    jnp.where(low_lanes, first, pltpu.roll(second, 64, 1)),
                    jnp.where(low_lanes, pltpu.roll(first, 64, 1), second),
                ]
                for first, second in turned
            ]
        )

    keeps = []
    for b in range(2):
        keep = lax.dot_general(
            mask_ref[b].astype(F32).astype(BF16),
            spread_ref[...],
            (COLS_COLS, ((), ())),
            preferred_element_type=F32,
        ).astype(BF16)
        keeps.append(square([[keep, keep], [keep, keep]]))

    partial = [partial_dft(jh) for jh in range(2)]
    twisted = [twist(value) for value in partial]
    spectrum = [split(product(split(value), rows(inner_f), ROWS_COLS)) for value in twisted]
    parts = [(b, jh) for b in range(2) for jh in range(2)]
    unwound = [
        product((spectrum[jh][0] * keeps[b], spectrum[jh][1] * keeps[b]), rows(inner_i), ROWS_COLS)
        for b, jh in parts
    ]
    untwisted = [untwist(value) for value in unwound]
    for (b, jh), value in zip(parts, untwisted):
        restored = product(rows(outer_i), split(value), ROWS_COLS)
        for th in range(2):
            for c in range(2):
                row = ((b * 2 + th) * 2 + c) * 2 + jh
                out_ref[pl.ds(row, 128, stride=16), :] = tile(restored, c, th)


def write_rows(out_ref, waves, sign_ref):
    for j in range(NPAIR):
        block = waves[j * HALF : (j + 1) * HALF, :]
        out_ref[CENTRE + j] = block
        if j:
            out_ref[CENTRE - j] = sign_ref[pl.ds(j, 1), :] * block


def waves_kernel(sign_ref, coef_ref, table_ref, kelvin_ref, mjo_ref):
    th = pl.program_id(0)
    table = (table_ref[0], table_ref[1])
    for b, out_ref in ((0, kelvin_ref), (1, mjo_ref)):
        row = (b * 2 + th) * 4
        coef = jnp.concatenate(
            [
                jnp.concatenate(
                    [coef_ref[pl.ds(row + c * 2 + jh, 128, stride=16), :] for jh in range(2)],
                    axis=1,
                )
                for c in range(2)
            ],
            axis=0,
        )
        write_rows(out_ref, product(split(coef), table, COLS_COLS), sign_ref)


def pick_kernel(coef_ref, own_ref, other_ref):
    level = lax.axis_index("lv")
    for out_ref, th in ((own_ref, level), (other_ref, 1 - level)):
        for r in range(4):
            out_ref[pl.ds(r * 128, 128), :] = coef_ref[pl.ds(8 + th * 4 + r, 128, stride=16), :]


def shear_kernel(sign_ref, own_ref, partner_ref, table_ref, out_ref):
    level_sign = jnp.where(lax.axis_index("lv") == 1, 1.0, -1.0)
    apart = level_sign * (own_ref[...] - partner_ref[...])
    coef = jnp.concatenate(
        [
            jnp.concatenate([apart[c * 256 : c * 256 + 128], apart[c * 256 + 128 : c * 256 + 256]], axis=1)
            for c in range(2)
        ],
        axis=0,
    )
    waves = product(split(coef), (table_ref[0], table_ref[1]), COLS_COLS)
    write_rows(out_ref, waves, sign_ref)


VMEM = pl.BlockSpec(memory_space=pltpu.VMEM)
HBM = pl.BlockSpec(memory_space=pltpu.HBM)


def call(kernel, in_specs, out_shapes, macs, moved, **kwargs):
    return pl.pallas_call(
        kernel,
        in_specs=in_specs,
        out_shape=out_shapes,
        cost_estimate=pl.CostEstimate(flops=2 * macs, bytes_accessed=moved, transcendentals=0),
        compiler_params=pltpu.CompilerParams(vmem_limit_bytes=32 << 20),
        **kwargs,
    )


def in_hbm(array):
    return pltpu.with_memory_space_constraint(array, pltpu.HBM)


def shape(*sizes):
    return jax.ShapeDtypeStruct(sizes, F32)


def body(wind_field, band_mask, sym_flag):
    record = jnp.transpose(wind_field[0], (1, 0, 2))
    outer_f, outer_i = outer_tables()
    inner_f, inner_i = inner_tables()
    spread = np.tile(np.eye(BLOCK), (1, 4)).astype(ml_dtypes.bfloat16)
    inverse_table = zonal_inverse_table()

    coef, signs = call(
        zonal_kernel,
        [HBM] * 3,
        (shape(1024, 128), shape(NPAIR, NLON)),
        3 * 512 * 360 * 256,
        3 << 20,
        out_specs=(VMEM, VMEM),
        scratch_shapes=[
            pltpu.SMEM((NPAIR,), jnp.int32),
            pltpu.VMEM((NLAT, BLOCK, NLON), F32),
            pltpu.VMEM((2, 2 * KM, NLON), BF16),
            pltpu.SemaphoreType.DMA((3,)),
        ],
    )(in_hbm(sym_flag), in_hbm(record), in_hbm(jnp.asarray(zonal_forward_table())))
    series = exchange(coef)
    filtered = call(
        time_kernel, [VMEM] * 8, shape(2048, 128), 3 * 4 * 512 * 256 * 256, 4 << 20, out_specs=VMEM
    )(
        series,
        band_mask.reshape(2, BLOCK, 128),
        spread,
        outer_f,
        inner_f,
        inner_i,
        outer_i,
        twist_tables(),
    )
    returned = exchange(filtered)
    own, other = call(
        pick_kernel, [VMEM], (shape(512, 128), shape(512, 128)), 1 << 10, 1 << 20, out_specs=(VMEM, VMEM)
    )(returned)
    partner = lax.ppermute(other, "lv", [(0, 1), (1, 0)])
    block = pl.BlockSpec((NLAT, HALF, NLON), lambda i: (0, i, 0))
    kelvin, mjo = call(
        waves_kernel,
        [VMEM, VMEM, VMEM],
        (shape(NLAT, BLOCK, NLON), shape(NLAT, BLOCK, NLON)),
        3 * 1024 * 360 * 256,
        5 << 20,
        grid=(2,),
        out_specs=(block, block),
    )(signs, returned, inverse_table)
    shear = call(
        shear_kernel, [VMEM] * 4, shape(NLAT, HALF, NLON), 3 * 256 * 360 * 256, 2 << 20, out_specs=VMEM
    )(signs, own, partner, inverse_table)
    return (
        jnp.transpose(kelvin, (1, 0, 2))[None],
        jnp.transpose(mjo, (1, 0, 2))[None],
        jnp.transpose(shear, (1, 0, 2)),
    )


def solution(mesh):
    placed = (P("lv", "ta", None, None), P(None, "ta", None), P())
    return jax.shard_map(
        body,
        mesh=mesh,
        in_specs=placed,
        out_specs=(
            P("lv", "ta", None, None),
            P("lv", "ta", None, None),
            P(("ta", "lv"), None, None),
        ),
        check_vma=False,
    )
```

```python
import functools

import jax
import jax.numpy as jnp
import ml_dtypes
import numpy as np
from jax import lax
from jax.experimental import pallas as pl
from jax.experimental.pallas import tpu as pltpu
from jax.sharding import PartitionSpec as P

NLON = 360
NLAT = 31
KM = 128
NT = 4096
NPAIR = 16
BLOCK = 32
HALF = 16
CENTRE = NPAIR - 1
FIRST_TURN = (2, 1, 4, 0)
SECOND_TURN = (2, 1, 4, 0)
F32 = jnp.float32
BF16 = jnp.bfloat16


def member_order(turn_by):
    index = np.arange(128).reshape(4, 2, 8, 2)
    return np.roll(index, turn_by, axis=(0, 1, 2, 3)).reshape(-1)


def exchange(blocks, turn_by):
    groups = [[int(member) for member in member_order(turn_by)]]
    return lax.all_to_all(
        blocks, "ta", split_axis=0, concat_axis=0, axis_index_groups=groups, tiled=True
    )


def halves(table):
    table = np.asarray(table, np.float32)
    high = table.astype(ml_dtypes.bfloat16)
    low = (table - high.astype(np.float32)).astype(ml_dtypes.bfloat16)
    return np.stack([high, low])


def turn(rows, cols, length):
    angle = 2.0 * np.pi / length * (np.outer(rows, cols) % length)
    return np.cos(angle), np.sin(angle)


def zonal_forward_table():
    cosine, sine = turn(member_order(FIRST_TURN), np.arange(NLON), NLON)
    return halves(np.concatenate([cosine, -sine]) / NLON)


def zonal_inverse_table():
    wavenumber = member_order(SECOND_TURN)
    cosine, sine = turn(wavenumber, np.arange(NLON), NLON)
    doubled = np.where(wavenumber == 0, 1.0, 2.0)[:, None]
    return halves(np.concatenate([cosine * doubled, -sine * doubled]))


def outer_tables():
    cosine, sine = turn(np.arange(128), member_order(FIRST_TURN), 128)
    forward = np.block([[cosine, sine], [-sine, cosine]])
    cosine, sine = turn(member_order(SECOND_TURN), np.arange(128), 128)
    inverse = np.block([[cosine, -sine], [sine, cosine]]) / NT
    return halves(forward), halves(inverse)


def inner_tables():
    cosine, sine = turn(np.arange(BLOCK), np.arange(BLOCK), BLOCK)
    eye = np.eye(4)
    cos4, sin4 = np.kron(eye, cosine), np.kron(eye, sine)
    forward = np.block([[cos4, -sin4], [sin4, cos4]])
    order = np.arange(128).reshape(4, 2, HALF).transpose(1, 0, 2).reshape(-1)
    cos4, sin4 = cos4[:, order], sin4[:, order]
    inverse = np.block([[cos4, sin4], [-sin4, cos4]])
    return halves(forward), halves(inverse)


def twist_tables():
    time = np.tile(np.arange(BLOCK), 4)
    order = np.arange(128).reshape(4, 2, HALF).transpose(1, 0, 2).reshape(-1)
    cosine, sine = turn(np.arange(128), time, NT)
    forward = np.stack([cosine, -sine])
    inverse = np.stack([cosine[:, order], sine[:, order]])
    return np.concatenate([forward, inverse]).astype(np.float32)


def split(value):
    high = value.astype(BF16)
    return high, (value - high.astype(F32)).astype(BF16)


def product(left, right, contract):
    dims = (contract, ((), ()))

    def dot(a, b):
        return lax.dot_general(a, b, dims, preferred_element_type=F32)

    return dot(left[0], right[0]) + (dot(left[0], right[1]) + dot(left[1], right[0]))


ROWS_COLS = ((1,), (0,))
ROWS_ROWS = ((1,), (1,))
COLS_COLS = ((0,), (0,))


def zonal_kernel(
    sym_hbm, wind_hbm, table_hbm, out_ref, sign_ref, sym_ref, wind_ref, table_ref, arrived
):
    loads = [
        pltpu.make_async_copy(source, target, arrived.at[i])
        for i, (source, target) in enumerate(
            ((sym_hbm, sym_ref), (wind_hbm, wind_ref), (table_hbm, table_ref))
        )
    ]
    for load in loads:
        load.start()
    for load in loads:
        load.wait()
    parts = []
    for j in range(NPAIR):
        sign = 1.0 - 2.0 * sym_ref[j].astype(F32)
        sign_ref[pl.ds(j, 1), :] = jnp.full((1, NLON), sign, F32)
        parts.append(0.5 * (wind_ref[CENTRE + j] + sign * wind_ref[CENTRE - j]))
    component = split(jnp.concatenate(parts, axis=0))
    coef = product((table_ref[0], table_ref[1]), component, ROWS_ROWS)
    for c in range(2):
        for jq in range(4):
            tile = coef[c * 128 : (c + 1) * 128, jq * 128 : (jq + 1) * 128]
            out_ref[pl.ds(c * 4 + jq, 128, stride=8), :] = tile


def time_kernel(
    series_ref, mask_ref, spread_ref, outer_f, inner_f, inner_i, outer_i, twist_ref, out_ref
):
    def rows(ref):
        return ref[0], ref[1]

    def tile(value, c, q):
        return value[c * 128 : (c + 1) * 128, q * 128 : (q + 1) * 128]

    def square(tiles):
        return jnp.concatenate([jnp.concatenate(row, axis=1) for row in tiles], axis=0)

    def partial_dft(jh):
        blocks = [
            [series_ref[pl.ds(c * 4 + jh * 2 + q, 128, stride=8), :] for q in range(2)]
            for c in range(2)
        ]
        return product(rows(outer_f), split(square(blocks)), ROWS_COLS)

    def twist(value):
        turned = []
        for q in range(2):
            real, imag = tile(value, 0, q), tile(value, 1, q)
            turned.append(
                [
                    real * twist_ref[0] - imag * twist_ref[1],
                    real * twist_ref[1] + imag * twist_ref[0],
                ]
            )
        return square(turned)

    low_lanes = lax.broadcasted_iota(jnp.int32, (128, 128), 1) < 64

    def untwist(value):
        turned = [[], []]
        for q in range(2):
            real, imag = tile(value, q, 0), tile(value, q, 1)
            turned[0].append(real * twist_ref[2] - imag * twist_ref[3])
            turned[1].append(real * twist_ref[3] + imag * twist_ref[2])
        return square(
            [
                [
                    jnp.where(low_lanes, first, pltpu.roll(second, 64, 1)),
                    jnp.where(low_lanes, pltpu.roll(first, 64, 1), second),
                ]
                for first, second in turned
            ]
        )

    keeps = []
    for b in range(2):
        keep = lax.dot_general(
            mask_ref[b].astype(F32).astype(BF16),
            spread_ref[...],
            (COLS_COLS, ((), ())),
            preferred_element_type=F32,
        ).astype(BF16)
        keeps.append(square([[keep, keep], [keep, keep]]))

    partial = [partial_dft(jh) for jh in range(2)]
    twisted = [twist(value) for value in partial]
    spectrum = [split(product(split(value), rows(inner_f), ROWS_COLS)) for value in twisted]
    parts = [(b, jh) for b in range(2) for jh in range(2)]
    unwound = [
        product((spectrum[jh][0] * keeps[b], spectrum[jh][1] * keeps[b]), rows(inner_i), ROWS_COLS)
        for b, jh in parts
    ]
    untwisted = [untwist(value) for value in unwound]
    for (b, jh), value in zip(parts, untwisted):
        restored = product(rows(outer_i), split(value), ROWS_COLS)
        for th in range(2):
            for c in range(2):
                row = ((b * 2 + th) * 2 + c) * 2 + jh
                out_ref[pl.ds(row, 128, stride=16), :] = tile(restored, c, th)


def write_rows(out_ref, waves, sign_ref):
    for j in range(NPAIR):
        block = waves[j * HALF : (j + 1) * HALF, :]
        out_ref[CENTRE + j] = block
        if j:
            out_ref[CENTRE - j] = sign_ref[pl.ds(j, 1), :] * block


def waves_kernel(sign_ref, coef_ref, table_ref, kelvin_ref, mjo_ref):
    th = pl.program_id(0)
    table = (table_ref[0], table_ref[1])
    for b, out_ref in ((0, kelvin_ref), (1, mjo_ref)):
        row = (b * 2 + th) * 4
        coef = jnp.concatenate(
            [
                jnp.concatenate(
                    [coef_ref[pl.ds(row + c * 2 + jh, 128, stride=16), :] for jh in range(2)],
                    axis=1,
                )
                for c in range(2)
            ],
            axis=0,
        )
        write_rows(out_ref, product(split(coef), table, COLS_COLS), sign_ref)


def pick_kernel(coef_ref, *out_refs):
    level = lax.axis_index("lv")
    for side, th in ((0, level), (1, 1 - level)):
        for jh in range(2):
            for c in range(2):
                out_refs[side * 2 + jh][pl.ds(c * 128, 128), :] = coef_ref[
                    pl.ds(8 + th * 4 + c * 2 + jh, 128, stride=16), :
                ]


def shear_kernel(jh, sign_ref, own_ref, partner_ref, table_ref, *rest):
    out_hbm, rows_ref, sent = rest[-3:]
    level_sign = jnp.where(lax.axis_index("lv") == 1, 1.0, -1.0)
    apart = level_sign * (own_ref[...] - partner_ref[...])
    waves = product(split(apart), (table_ref[0], table_ref[1]), COLS_COLS)
    centre = (7, 15)[jh]
    for i in range(8):
        j = jh * 8 + i
        block = waves[i * HALF : (i + 1) * HALF, :]
        rows_ref[7 + i + jh] = block
        if j:
            rows_ref[centre - j] = sign_ref[pl.ds(j, 1), :] * block
    stores = [
        pltpu.make_async_copy(
            rows_ref.at[pl.ds(source, count)], out_hbm.at[pl.ds(target, count)], sent.at[i]
        )
        for i, (source, target, count) in enumerate((((0, 8, 15),), ((0, 0, 8), (8, 23, 8)))[jh])
    ]
    for store in stores:
        store.start()
    for store in stores:
        store.wait()


VMEM = pl.BlockSpec(memory_space=pltpu.VMEM)
HBM = pl.BlockSpec(memory_space=pltpu.HBM)


def call(kernel, in_specs, out_shapes, macs, moved, **kwargs):
    return pl.pallas_call(
        kernel,
        in_specs=in_specs,
        out_shape=out_shapes,
        cost_estimate=pl.CostEstimate(flops=2 * macs, bytes_accessed=moved, transcendentals=0),
        compiler_params=pltpu.CompilerParams(vmem_limit_bytes=32 << 20),
        **kwargs,
    )


def in_hbm(array):
    return pltpu.with_memory_space_constraint(array, pltpu.HBM)


def shape(*sizes):
    return jax.ShapeDtypeStruct(sizes, F32)


def body(wind_field, band_mask, sym_flag):
    record = jnp.transpose(wind_field[0], (1, 0, 2))
    outer_f, outer_i = outer_tables()
    inner_f, inner_i = inner_tables()
    spread = np.tile(np.eye(BLOCK), (1, 4)).astype(ml_dtypes.bfloat16)
    inverse_table = zonal_inverse_table()

    coef, signs = call(
        zonal_kernel,
        [HBM] * 3,
        (shape(1024, 128), shape(NPAIR, NLON)),
        3 * 512 * 360 * 256,
        3 << 20,
        out_specs=(VMEM, VMEM),
        scratch_shapes=[
            pltpu.SMEM((NPAIR,), jnp.int32),
            pltpu.VMEM((NLAT, BLOCK, NLON), F32),
            pltpu.VMEM((2, 2 * KM, NLON), BF16),
            pltpu.SemaphoreType.DMA((3,)),
        ],
    )(in_hbm(sym_flag), in_hbm(record), in_hbm(jnp.asarray(zonal_forward_table())))
    series = exchange(coef, FIRST_TURN)
    filtered = call(
        time_kernel, [VMEM] * 8, shape(2048, 128), 3 * 4 * 512 * 256 * 256, 4 << 20, out_specs=VMEM
    )(
        series,
        band_mask.reshape(2, BLOCK, 128),
        spread,
        outer_f,
        inner_f,
        inner_i,
        outer_i,
        twist_tables(),
    )
    returned = exchange(filtered, SECOND_TURN)
    picked = call(
        pick_kernel, [VMEM], (shape(256, 128),) * 4, 1 << 10, 1 << 20, out_specs=(VMEM,) * 4
    )(returned)
    partner = [lax.ppermute(other, "lv", [(0, 1), (1, 0)]) for other in picked[2:]]
    block = pl.BlockSpec((NLAT, HALF, NLON), lambda i: (0, i, 0))
    kelvin, mjo = call(
        waves_kernel,
        [VMEM, VMEM, VMEM],
        (shape(NLAT, BLOCK, NLON), shape(NLAT, BLOCK, NLON)),
        3 * 1024 * 360 * 256,
        5 << 20,
        grid=(2,),
        out_specs=(block, block),
    )(signs, returned, inverse_table)
    shear = []
    for jh in range(2):
        shear = [
            call(
                functools.partial(shear_kernel, jh),
                [VMEM] * 4 + [HBM] * jh,
                shape(NLAT, HALF, NLON),
                3 * 128 * 360 * 256,
                1 << 20,
                out_specs=HBM,
                scratch_shapes=[
                    pltpu.VMEM((16, HALF, NLON), F32),
                    pltpu.SemaphoreType.DMA((2,)),
                ],
                input_output_aliases={4: 0} if jh else {},
            )(signs, picked[jh], partner[jh], inverse_table, *shear)
        ]
    return (
        jnp.transpose(kelvin, (1, 0, 2))[None],
        jnp.transpose(mjo, (1, 0, 2))[None],
        jnp.transpose(shear[0], (1, 0, 2)),
    )


def solution(mesh):
    placed = (P("lv", "ta", None, None), P(None, "ta", None), P())
    return jax.shard_map(
        body,
        mesh=mesh,
        in_specs=placed,
        out_specs=(
            P("lv", "ta", None, None),
            P("lv", "ta", None, None),
            P(("ta", "lv"), None, None),
        ),
        check_vma=False,
    )
```

```python
import functools

import jax
import jax.numpy as jnp
import ml_dtypes
import numpy as np
from jax import lax
from jax.experimental import pallas as pl
from jax.experimental.pallas import tpu as pltpu
from jax.sharding import PartitionSpec as P

NLON = 360
NLAT = 31
KM = 128
NT = 4096
NPAIR = 16
BLOCK = 32
HALF = 16
CENTRE = NPAIR - 1
FIRST_TURN = (2, 1, 4, 1)
SECOND_TURN = (2, 1, 4, 1)
F32 = jnp.float32
BF16 = jnp.bfloat16


def member_order(turn_by):
    index = np.arange(128).reshape(4, 2, 8, 2)
    return np.roll(index, turn_by, axis=(0, 1, 2, 3)).reshape(-1)


def exchange(blocks, turn_by):
    groups = [[int(member) for member in member_order(turn_by)]]
    return lax.all_to_all(
        blocks, "ta", split_axis=0, concat_axis=0, axis_index_groups=groups, tiled=True
    )


def halves(table):
    table = np.asarray(table, np.float32)
    high = table.astype(ml_dtypes.bfloat16)
    low = (table - high.astype(np.float32)).astype(ml_dtypes.bfloat16)
    return np.stack([high, low])


def turn(rows, cols, length):
    angle = 2.0 * np.pi / length * (np.outer(rows, cols) % length)
    return np.cos(angle), np.sin(angle)


def zonal_forward_table():
    cosine, sine = turn(member_order(FIRST_TURN), np.arange(NLON), NLON)
    return halves(np.concatenate([cosine, -sine]) / NLON)


def zonal_inverse_table():
    wavenumber = member_order(SECOND_TURN)
    cosine, sine = turn(wavenumber, np.arange(NLON), NLON)
    doubled = np.where(wavenumber == 0, 1.0, 2.0)[:, None]
    return halves(np.concatenate([cosine * doubled, -sine * doubled]))


def outer_tables():
    cosine, sine = turn(np.arange(128), member_order(FIRST_TURN), 128)
    forward = np.block([[cosine, sine], [-sine, cosine]])
    cosine, sine = turn(member_order(SECOND_TURN), np.arange(128), 128)
    inverse = np.block([[cosine, -sine], [sine, cosine]]) / NT
    return halves(forward), halves(inverse)


def inner_tables():
    cosine, sine = turn(np.arange(BLOCK), np.arange(BLOCK), BLOCK)
    eye = np.eye(4)
    cos4, sin4 = np.kron(eye, cosine), np.kron(eye, sine)
    forward = np.block([[cos4, -sin4], [sin4, cos4]])
    order = np.arange(128).reshape(4, 2, HALF).transpose(1, 0, 2).reshape(-1)
    cos4, sin4 = cos4[:, order], sin4[:, order]
    inverse = np.block([[cos4, sin4], [-sin4, cos4]])
    return halves(forward), halves(inverse)


def twist_tables():
    time = np.tile(np.arange(BLOCK), 4)
    order = np.arange(128).reshape(4, 2, HALF).transpose(1, 0, 2).reshape(-1)
    cosine, sine = turn(np.arange(128), time, NT)
    forward = np.stack([cosine, -sine])
    inverse = np.stack([cosine[:, order], sine[:, order]])
    return np.concatenate([forward, inverse]).astype(np.float32)


def split(value):
    high = value.astype(BF16)
    return high, (value - high.astype(F32)).astype(BF16)


def product(left, right, contract):
    dims = (contract, ((), ()))

    def dot(a, b):
        return lax.dot_general(a, b, dims, preferred_element_type=F32)

    return dot(left[0], right[0]) + (dot(left[0], right[1]) + dot(left[1], right[0]))


ROWS_COLS = ((1,), (0,))
ROWS_ROWS = ((1,), (1,))
COLS_COLS = ((0,), (0,))


def zonal_kernel(
    sym_hbm, wind_hbm, table_hbm, out_ref, sign_ref, sym_ref, wind_ref, table_ref, arrived
):
    loads = [
        pltpu.make_async_copy(source, target, arrived.at[i])
        for i, (source, target) in enumerate(
            ((sym_hbm, sym_ref), (wind_hbm, wind_ref), (table_hbm, table_ref))
        )
    ]
    for load in loads:
        load.start()
    for load in loads:
        load.wait()
    parts = []
    for j in range(NPAIR):
        sign = 1.0 - 2.0 * sym_ref[j].astype(F32)
        sign_ref[pl.ds(j, 1), :] = jnp.full((1, NLON), sign, F32)
        parts.append(0.5 * (wind_ref[CENTRE + j] + sign * wind_ref[CENTRE - j]))
    component = split(jnp.concatenate(parts, axis=0))
    coef = product((table_ref[0], table_ref[1]), component, ROWS_ROWS)
    for c in range(2):
        for jq in range(4):
            tile = coef[c * 128 : (c + 1) * 128, jq * 128 : (jq + 1) * 128]
            out_ref[pl.ds(c * 4 + jq, 128, stride=8), :] = tile


def time_kernel(
    series_ref, mask_ref, spread_ref, outer_f, inner_f, inner_i, outer_i, twist_ref, out_ref
):
    def rows(ref):
        return ref[0], ref[1]

    def tile(value, c, q):
        return value[c * 128 : (c + 1) * 128, q * 128 : (q + 1) * 128]

    def square(tiles):
        return jnp.concatenate([jnp.concatenate(row, axis=1) for row in tiles], axis=0)

    def partial_dft(jh):
        blocks = [
            [series_ref[pl.ds(c * 4 + jh * 2 + q, 128, stride=8), :] for q in range(2)]
            for c in range(2)
        ]
        return product(rows(outer_f), split(square(blocks)), ROWS_COLS)

    def twist(value):
        turned = []
        for q in range(2):
            real, imag = tile(value, 0, q), tile(value, 1, q)
            turned.append(
                [
                    real * twist_ref[0] - imag * twist_ref[1],
                    real * twist_ref[1] + imag * twist_ref[0],
                ]
            )
        return square(turned)

    low_lanes = lax.broadcasted_iota(jnp.int32, (128, 128), 1) < 64

    def untwist(value):
        turned = [[], []]
        for q in range(2):
            real, imag = tile(value, q, 0), tile(value, q, 1)
            turned[0].append(real * twist_ref[2] - imag * twist_ref[3])
            turned[1].append(real * twist_ref[3] + imag * twist_ref[2])
        return square(
            [
                [
                    jnp.where(low_lanes, first, pltpu.roll(second, 64, 1)),
                    jnp.where(low_lanes, pltpu.roll(first, 64, 1), second),
                ]
                for first, second in turned
            ]
        )

    keeps = []
    for b in range(2):
        keep = lax.dot_general(
            mask_ref[b].astype(F32).astype(BF16),
            spread_ref[...],
            (COLS_COLS, ((), ())),
            preferred_element_type=F32,
        ).astype(BF16)
        keeps.append(square([[keep, keep], [keep, keep]]))

    partial = [partial_dft(jh) for jh in range(2)]
    twisted = [twist(value) for value in partial]
    spectrum = [split(product(split(value), rows(inner_f), ROWS_COLS)) for value in twisted]
    parts = [(b, jh) for b in range(2) for jh in range(2)]
    unwound = [
        product((spectrum[jh][0] * keeps[b], spectrum[jh][1] * keeps[b]), rows(inner_i), ROWS_COLS)
        for b, jh in parts
    ]
    untwisted = [untwist(value) for value in unwound]
    for (b, jh), value in zip(parts, untwisted):
        restored = product(rows(outer_i), split(value), ROWS_COLS)
        for th in range(2):
            for c in range(2):
                row = ((b * 2 + th) * 2 + c) * 2 + jh
                out_ref[pl.ds(row, 128, stride=16), :] = tile(restored, c, th)


def write_rows(out_ref, waves, sign_ref):
    for j in range(NPAIR):
        block = waves[j * HALF : (j + 1) * HALF, :]
        out_ref[CENTRE + j] = block
        if j:
            out_ref[CENTRE - j] = sign_ref[pl.ds(j, 1), :] * block


def waves_kernel(sign_ref, coef_ref, table_ref, kelvin_ref, mjo_ref):
    th = pl.program_id(0)
    table = (table_ref[0], table_ref[1])
    for b, out_ref in ((0, kelvin_ref), (1, mjo_ref)):
        row = (b * 2 + th) * 4
        coef = jnp.concatenate(
            [
                jnp.concatenate(
                    [coef_ref[pl.ds(row + c * 2 + jh, 128, stride=16), :] for jh in range(2)],
                    axis=1,
                )
                for c in range(2)
            ],
            axis=0,
        )
        write_rows(out_ref, product(split(coef), table, COLS_COLS), sign_ref)


def pick_kernel(coef_ref, *out_refs):
    level = lax.axis_index("lv")
    for side, th in ((0, level), (1, 1 - level)):
        for jh in range(2):
            for c in range(2):
                out_refs[side * 2 + jh][pl.ds(c * 128, 128), :] = coef_ref[
                    pl.ds(8 + th * 4 + c * 2 + jh, 128, stride=16), :
                ]


def shear_kernel(jh, sign_ref, own_ref, partner_ref, table_ref, *rest):
    out_hbm, rows_ref, sent = rest[-3:]
    level_sign = jnp.where(lax.axis_index("lv") == 1, 1.0, -1.0)
    apart = level_sign * (own_ref[...] - partner_ref[...])
    waves = product(split(apart), (table_ref[0], table_ref[1]), COLS_COLS)
    centre = (7, 15)[jh]
    for i in range(8):
        j = jh * 8 + i
        block = waves[i * HALF : (i + 1) * HALF, :]
        rows_ref[7 + i + jh] = block
        if j:
            rows_ref[centre - j] = sign_ref[pl.ds(j, 1), :] * block
    stores = [
        pltpu.make_async_copy(
            rows_ref.at[pl.ds(source, count)], out_hbm.at[pl.ds(target, count)], sent.at[i]
        )
        for i, (source, target, count) in enumerate((((0, 8, 15),), ((0, 0, 8), (8, 23, 8)))[jh])
    ]
    for store in stores:
        store.start()
    for store in stores:
        store.wait()


VMEM = pl.BlockSpec(memory_space=pltpu.VMEM)
HBM = pl.BlockSpec(memory_space=pltpu.HBM)


def call(kernel, in_specs, out_shapes, macs, moved, **kwargs):
    return pl.pallas_call(
        kernel,
        in_specs=in_specs,
        out_shape=out_shapes,
        cost_estimate=pl.CostEstimate(flops=2 * macs, bytes_accessed=moved, transcendentals=0),
        compiler_params=pltpu.CompilerParams(vmem_limit_bytes=32 << 20),
        **kwargs,
    )


def in_hbm(array):
    return pltpu.with_memory_space_constraint(array, pltpu.HBM)


def shape(*sizes):
    return jax.ShapeDtypeStruct(sizes, F32)


def body(wind_field, band_mask, sym_flag):
    record = jnp.transpose(wind_field[0], (1, 0, 2))
    outer_f, outer_i = outer_tables()
    inner_f, inner_i = inner_tables()
    spread = np.tile(np.eye(BLOCK), (1, 4)).astype(ml_dtypes.bfloat16)
    inverse_table = zonal_inverse_table()

    coef, signs = call(
        zonal_kernel,
        [HBM] * 3,
        (shape(1024, 128), shape(NPAIR, NLON)),
        3 * 512 * 360 * 256,
        3 << 20,
        out_specs=(VMEM, VMEM),
        scratch_shapes=[
            pltpu.SMEM((NPAIR,), jnp.int32),
            pltpu.VMEM((NLAT, BLOCK, NLON), F32),
            pltpu.VMEM((2, 2 * KM, NLON), BF16),
            pltpu.SemaphoreType.DMA((3,)),
        ],
    )(in_hbm(sym_flag), in_hbm(record), in_hbm(jnp.asarray(zonal_forward_table())))
    series = exchange(coef, FIRST_TURN)
    filtered = call(
        time_kernel, [VMEM] * 8, shape(2048, 128), 3 * 4 * 512 * 256 * 256, 4 << 20, out_specs=VMEM
    )(
        series,
        band_mask.reshape(2, BLOCK, 128),
        spread,
        outer_f,
        inner_f,
        inner_i,
        outer_i,
        twist_tables(),
    )
    returned = exchange(filtered, SECOND_TURN)
    picked = call(
        pick_kernel, [VMEM], (shape(256, 128),) * 4, 1 << 10, 1 << 20, out_specs=(VMEM,) * 4
    )(returned)
    partner = [lax.ppermute(other, "lv", [(0, 1), (1, 0)]) for other in picked[2:]]
    block = pl.BlockSpec((NLAT, HALF, NLON), lambda i: (0, i, 0))
    kelvin, mjo = call(
        waves_kernel,
        [VMEM, VMEM, VMEM],
        (shape(NLAT, BLOCK, NLON), shape(NLAT, BLOCK, NLON)),
        3 * 1024 * 360 * 256,
        5 << 20,
        grid=(2,),
        out_specs=(block, block),
    )(signs, returned, inverse_table)
    shear = []
    for jh in range(2):
        shear = [
            call(
                functools.partial(shear_kernel, jh),
                [VMEM] * 4 + [HBM] * jh,
                shape(NLAT, HALF, NLON),
                3 * 128 * 360 * 256,
                1 << 20,
                out_specs=HBM,
                scratch_shapes=[
                    pltpu.VMEM((16, HALF, NLON), F32),
                    pltpu.SemaphoreType.DMA((2,)),
                ],
                input_output_aliases={4: 0} if jh else {},
            )(signs, picked[jh], partner[jh], inverse_table, *shear)
        ]
    return (
        jnp.transpose(kelvin, (1, 0, 2))[None],
        jnp.transpose(mjo, (1, 0, 2))[None],
        jnp.transpose(shear[0], (1, 0, 2)),
    )


def solution(mesh):
    placed = (P("lv", "ta", None, None), P(None, "ta", None), P())
    return jax.shard_map(
        body,
        mesh=mesh,
        in_specs=placed,
        out_specs=(
            P("lv", "ta", None, None),
            P("lv", "ta", None, None),
            P(("ta", "lv"), None, None),
        ),
        check_vma=False,
    )
```

```python
import functools

import jax
import jax.numpy as jnp
import ml_dtypes
import numpy as np
from jax import lax
from jax.experimental import pallas as pl
from jax.experimental.pallas import tpu as pltpu
from jax.sharding import PartitionSpec as P

NLON = 360
NLAT = 31
KM = 128
NT = 4096
NPAIR = 16
BLOCK = 32
HALF = 16
CENTRE = NPAIR - 1
FIRST_TURN = (2, 1, 4, 1)
SECOND_TURN = (2, 1, 4, 1)
F32 = jnp.float32
BF16 = jnp.bfloat16


def member_order(turn_by):
    index = np.arange(128).reshape(4, 2, 8, 2)
    return np.roll(index, turn_by, axis=(0, 1, 2, 3)).reshape(-1)


def exchange(blocks, turn_by):
    groups = [[int(member) for member in member_order(turn_by)]]
    return lax.all_to_all(
        blocks, "ta", split_axis=0, concat_axis=0, axis_index_groups=groups, tiled=True
    )


def halves(table):
    table = np.asarray(table, np.float32)
    high = table.astype(ml_dtypes.bfloat16)
    low = (table - high.astype(np.float32)).astype(ml_dtypes.bfloat16)
    return np.stack([high, low])


def turn(rows, cols, length):
    angle = 2.0 * np.pi / length * (np.outer(rows, cols) % length)
    return np.cos(angle), np.sin(angle)


def zonal_forward_table():
    cosine, sine = turn(member_order(FIRST_TURN), np.arange(NLON), NLON)
    return halves(np.concatenate([cosine, -sine]) / NLON)


def zonal_inverse_table():
    wavenumber = member_order(SECOND_TURN)
    cosine, sine = turn(wavenumber, np.arange(NLON), NLON)
    doubled = np.where(wavenumber == 0, 1.0, 2.0)[:, None]
    return halves(np.concatenate([cosine * doubled, -sine * doubled]))


def outer_tables():
    cosine, sine = turn(np.arange(128), member_order(FIRST_TURN), 128)
    forward = np.block([[cosine, sine], [-sine, cosine]])
    cosine, sine = turn(member_order(SECOND_TURN), np.arange(128), 128)
    inverse = np.block([[cosine, -sine], [sine, cosine]]) / NT
    return halves(forward), halves(inverse)


def inner_tables():
    cosine, sine = turn(np.arange(BLOCK), np.arange(BLOCK), BLOCK)
    eye = np.eye(4)
    cos4, sin4 = np.kron(eye, cosine), np.kron(eye, sine)
    forward = np.block([[cos4, -sin4], [sin4, cos4]])
    order = np.arange(128).reshape(4, 2, HALF).transpose(1, 0, 2).reshape(-1)
    cos4, sin4 = cos4[:, order], sin4[:, order]
    inverse = np.block([[cos4, sin4], [-sin4, cos4]])
    return halves(forward), halves(inverse)


def twist_tables():
    time = np.tile(np.arange(BLOCK), 4)
    order = np.arange(128).reshape(4, 2, HALF).transpose(1, 0, 2).reshape(-1)
    cosine, sine = turn(np.arange(128), time, NT)
    forward = np.stack([cosine, -sine])
    inverse = np.stack([cosine[:, order], sine[:, order]])
    return np.concatenate([forward, inverse]).astype(np.float32)


def split(value):
    high = value.astype(BF16)
    return high, (value - high.astype(F32)).astype(BF16)


def product(left, right, contract):
    dims = (contract, ((), ()))

    def dot(a, b):
        return lax.dot_general(a, b, dims, preferred_element_type=F32)

    return dot(left[0], right[0]) + (dot(left[0], right[1]) + dot(left[1], right[0]))


ROWS_COLS = ((1,), (0,))
ROWS_ROWS = ((1,), (1,))
COLS_COLS = ((0,), (0,))


def zonal_kernel(
    sym_hbm, wind_hbm, table_hbm, out_ref, sign_ref, sym_ref, wind_ref, table_ref, arrived
):
    cuts = (pl.ds(0, 256), pl.ds(256, NLON - 256))
    flags = pltpu.make_async_copy(sym_hbm, sym_ref, arrived.at[0])
    flags.start()
    loads = []
    for i, cut in enumerate(cuts):
        pair = [
            pltpu.make_async_copy(
                source.at[:, :, cut], target.at[:, :, cut], arrived.at[1 + 2 * i + n]
            )
            for n, (source, target) in enumerate(((wind_hbm, wind_ref), (table_hbm, table_ref)))
        ]
        for load in pair:
            load.start()
        loads.append(pair)
    flags.wait()
    signs = [1.0 - 2.0 * sym_ref[j].astype(F32) for j in range(NPAIR)]
    for j in range(NPAIR):
        sign_ref[pl.ds(j, 1), :] = jnp.full((1, NLON), signs[j], F32)
    terms = []
    for cut, pair in zip(cuts, loads):
        for load in pair:
            load.wait()
        component = jnp.concatenate(
            [
                0.5 * (wind_ref[CENTRE + j, :, cut] + signs[j] * wind_ref[CENTRE - j, :, cut])
                for j in range(NPAIR)
            ],
            axis=0,
        )
        table = (table_ref[0, :, cut], table_ref[1, :, cut])
        terms.append(product(table, split(component), ROWS_ROWS))
    coef = terms[0] + terms[1]
    for c in range(2):
        for jq in range(4):
            tile = coef[c * 128 : (c + 1) * 128, jq * 128 : (jq + 1) * 128]
            out_ref[pl.ds(c * 4 + jq, 128, stride=8), :] = tile


def time_kernel(
    series_ref, mask_ref, spread_ref, outer_f, inner_f, inner_i, outer_i, twist_ref, out_ref
):
    def rows(ref):
        return ref[0], ref[1]

    def tile(value, c, q):
        return value[c * 128 : (c + 1) * 128, q * 128 : (q + 1) * 128]

    def square(tiles):
        return jnp.concatenate([jnp.concatenate(row, axis=1) for row in tiles], axis=0)

    def partial_dft(jh):
        blocks = [
            [series_ref[pl.ds(c * 4 + jh * 2 + q, 128, stride=8), :] for q in range(2)]
            for c in range(2)
        ]
        return product(rows(outer_f), split(square(blocks)), ROWS_COLS)

    def twist(value):
        turned = []
        for q in range(2):
            real, imag = tile(value, 0, q), tile(value, 1, q)
            turned.append(
                [
                    real * twist_ref[0] - imag * twist_ref[1],
                    real * twist_ref[1] + imag * twist_ref[0],
                ]
            )
        return square(turned)

    low_lanes = lax.broadcasted_iota(jnp.int32, (128, 128), 1) < 64

    def untwist(value):
        turned = [[], []]
        for q in range(2):
            real, imag = tile(value, q, 0), tile(value, q, 1)
            turned[0].append(real * twist_ref[2] - imag * twist_ref[3])
            turned[1].append(real * twist_ref[3] + imag * twist_ref[2])
        return square(
            [
                [
                    jnp.where(low_lanes, first, pltpu.roll(second, 64, 1)),
                    jnp.where(low_lanes, pltpu.roll(first, 64, 1), second),
                ]
                for first, second in turned
            ]
        )

    keeps = []
    for b in range(2):
        keep = lax.dot_general(
            mask_ref[b].astype(F32).astype(BF16),
            spread_ref[...],
            (COLS_COLS, ((), ())),
            preferred_element_type=F32,
        ).astype(BF16)
        keeps.append(square([[keep, keep], [keep, keep]]))

    partial = [partial_dft(jh) for jh in range(2)]
    twisted = [twist(value) for value in partial]
    spectrum = [split(product(split(value), rows(inner_f), ROWS_COLS)) for value in twisted]
    parts = [(b, jh) for b in range(2) for jh in range(2)]
    unwound = [
        product((spectrum[jh][0] * keeps[b], spectrum[jh][1] * keeps[b]), rows(inner_i), ROWS_COLS)
        for b, jh in parts
    ]
    untwisted = [untwist(value) for value in unwound]
    for (b, jh), value in zip(parts, untwisted):
        restored = product(rows(outer_i), split(value), ROWS_COLS)
        for th in range(2):
            for c in range(2):
                row = ((b * 2 + th) * 2 + c) * 2 + jh
                out_ref[pl.ds(row, 128, stride=16), :] = tile(restored, c, th)


def write_rows(out_ref, waves, sign_ref):
    for j in range(NPAIR):
        block = waves[j * HALF : (j + 1) * HALF, :]
        out_ref[CENTRE + j] = block
        if j:
            out_ref[CENTRE - j] = sign_ref[pl.ds(j, 1), :] * block


def waves_kernel(sign_ref, coef_ref, table_ref, kelvin_ref, mjo_ref):
    th = pl.program_id(0)
    table = (table_ref[0], table_ref[1])
    for b, out_ref in ((0, kelvin_ref), (1, mjo_ref)):
        row = (b * 2 + th) * 4
        coef = jnp.concatenate(
            [
                jnp.concatenate(
                    [coef_ref[pl.ds(row + c * 2 + jh, 128, stride=16), :] for jh in range(2)],
                    axis=1,
                )
                for c in range(2)
            ],
            axis=0,
        )
        write_rows(out_ref, product(split(coef), table, COLS_COLS), sign_ref)


def pick_kernel(coef_ref, *out_refs):
    first = 8 + (1 - lax.axis_index("lv")) * 4
    for jh, out_ref in enumerate(out_refs):
        for c in range(2):
            out_ref[pl.ds(c * 128, 128), :] = coef_ref[pl.ds(first + c * 2 + jh, 128, stride=16), :]


def shear_kernel(jh, sign_ref, coef_ref, partner_ref, table_ref, *rest):
    out_hbm, rows_ref, sent = rest[-3:]
    level = lax.axis_index("lv")
    level_sign = jnp.where(level == 1, 1.0, -1.0)
    own = jnp.concatenate(
        [coef_ref[pl.ds(8 + level * 4 + c * 2 + jh, 128, stride=16), :] for c in range(2)], axis=0
    )
    apart = level_sign * (own - partner_ref[...])
    waves = product(split(apart), (table_ref[0], table_ref[1]), COLS_COLS)
    centre = (7, 15)[jh]
    for i in range(8):
        j = jh * 8 + i
        block = waves[i * HALF : (i + 1) * HALF, :]
        rows_ref[7 + i + jh] = block
        if j:
            rows_ref[centre - j] = sign_ref[pl.ds(j, 1), :] * block
    stores = [
        pltpu.make_async_copy(
            rows_ref.at[pl.ds(source, count)], out_hbm.at[pl.ds(target, count)], sent.at[i]
        )
        for i, (source, target, count) in enumerate((((0, 8, 15),), ((0, 0, 8), (8, 23, 8)))[jh])
    ]
    for store in stores:
        store.start()
    for store in stores:
        store.wait()


VMEM = pl.BlockSpec(memory_space=pltpu.VMEM)
HBM = pl.BlockSpec(memory_space=pltpu.HBM)


def call(kernel, in_specs, out_shapes, macs, moved, **kwargs):
    return pl.pallas_call(
        kernel,
        in_specs=in_specs,
        out_shape=out_shapes,
        cost_estimate=pl.CostEstimate(flops=2 * macs, bytes_accessed=moved, transcendentals=0),
        compiler_params=pltpu.CompilerParams(vmem_limit_bytes=32 << 20),
        **kwargs,
    )


def in_hbm(array):
    return pltpu.with_memory_space_constraint(array, pltpu.HBM)


def shape(*sizes):
    return jax.ShapeDtypeStruct(sizes, F32)


def body(wind_field, band_mask, sym_flag):
    record = jnp.transpose(wind_field[0], (1, 0, 2))
    outer_f, outer_i = outer_tables()
    inner_f, inner_i = inner_tables()
    spread = np.tile(np.eye(BLOCK), (1, 4)).astype(ml_dtypes.bfloat16)
    inverse_table = zonal_inverse_table()

    coef, signs = call(
        zonal_kernel,
        [HBM] * 3,
        (shape(1024, 128), shape(NPAIR, NLON)),
        3 * 512 * 360 * 256,
        3 << 20,
        out_specs=(VMEM, VMEM),
        scratch_shapes=[
            pltpu.SMEM((NPAIR,), jnp.int32),
            pltpu.VMEM((NLAT, BLOCK, NLON), F32),
            pltpu.VMEM((2, 2 * KM, NLON), BF16),
            pltpu.SemaphoreType.DMA((5,)),
        ],
    )(in_hbm(sym_flag), in_hbm(record), in_hbm(jnp.asarray(zonal_forward_table())))
    series = exchange(coef, FIRST_TURN)
    filtered = call(
        time_kernel, [VMEM] * 8, shape(2048, 128), 3 * 4 * 512 * 256 * 256, 4 << 20, out_specs=VMEM
    )(
        series,
        band_mask.reshape(2, BLOCK, 128),
        spread,
        outer_f,
        inner_f,
        inner_i,
        outer_i,
        twist_tables(),
    )
    returned = exchange(filtered, SECOND_TURN)
    picked = call(
        pick_kernel, [VMEM], (shape(256, 128),) * 2, 1 << 10, 1 << 20, out_specs=(VMEM,) * 2
    )(returned)
    partner = [lax.ppermute(other, "lv", [(0, 1), (1, 0)]) for other in picked]
    block = pl.BlockSpec((NLAT, HALF, NLON), lambda i: (0, i, 0))
    kelvin, mjo = call(
        waves_kernel,
        [VMEM, VMEM, VMEM],
        (shape(NLAT, BLOCK, NLON), shape(NLAT, BLOCK, NLON)),
        3 * 1024 * 360 * 256,
        5 << 20,
        grid=(2,),
        out_specs=(block, block),
    )(signs, returned, inverse_table)
    shear = []
    for jh in range(2):
        shear = [
            call(
                functools.partial(shear_kernel, jh),
                [VMEM] * 4 + [HBM] * jh,
                shape(NLAT, HALF, NLON),
                3 * 128 * 360 * 256,
                1 << 20,
                out_specs=HBM,
                scratch_shapes=[
                    pltpu.VMEM((16, HALF, NLON), F32),
                    pltpu.SemaphoreType.DMA((2,)),
                ],
                input_output_aliases={4: 0} if jh else {},
            )(signs, returned, partner[jh], inverse_table, *shear)
        ]
    return (
        jnp.transpose(kelvin, (1, 0, 2))[None],
        jnp.transpose(mjo, (1, 0, 2))[None],
        jnp.transpose(shear[0], (1, 0, 2)),
    )


def solution(mesh):
    placed = (P("lv", "ta", None, None), P(None, "ta", None), P())
    return jax.shard_map(
        body,
        mesh=mesh,
        in_specs=placed,
        out_specs=(
            P("lv", "ta", None, None),
            P("lv", "ta", None, None),
            P(("ta", "lv"), None, None),
        ),
        check_vma=False,
    )
```

```python
import functools

import jax
import jax.numpy as jnp
import ml_dtypes
import numpy as np
from jax import lax
from jax.experimental import pallas as pl
from jax.experimental.pallas import tpu as pltpu
from jax.sharding import PartitionSpec as P

NLON = 360
NLAT = 31
KM = 128
NT = 4096
NPAIR = 16
BLOCK = 32
HALF = 16
CENTRE = NPAIR - 1
FIRST_TURN = (2, 1, 4, 1)
SECOND_TURN = (2, 1, 4, 1)
F32 = jnp.float32
BF16 = jnp.bfloat16


def member_order(turn_by):
    index = np.arange(128).reshape(4, 2, 8, 2)
    return np.roll(index, turn_by, axis=(0, 1, 2, 3)).reshape(-1)


def exchange(blocks, turn_by):
    groups = [[int(member) for member in member_order(turn_by)]]
    return lax.all_to_all(
        blocks, "ta", split_axis=0, concat_axis=0, axis_index_groups=groups, tiled=True
    )


def halves(table):
    table = np.asarray(table, np.float32)
    high = table.astype(ml_dtypes.bfloat16)
    low = (table - high.astype(np.float32)).astype(ml_dtypes.bfloat16)
    return np.stack([high, low])


def turn(rows, cols, length):
    angle = 2.0 * np.pi / length * (np.outer(rows, cols) % length)
    return np.cos(angle), np.sin(angle)


def zonal_forward_table():
    cosine, sine = turn(member_order(FIRST_TURN), np.arange(NLON), NLON)
    return halves(np.concatenate([cosine, -sine]) / NLON)


def zonal_inverse_table():
    wavenumber = member_order(SECOND_TURN)
    cosine, sine = turn(wavenumber, np.arange(NLON), NLON)
    doubled = np.where(wavenumber == 0, 1.0, 2.0)[:, None]
    return halves(np.concatenate([cosine * doubled, -sine * doubled]))


def outer_tables():
    cosine, sine = turn(np.arange(128), member_order(FIRST_TURN), 128)
    forward = np.block([[cosine, sine], [-sine, cosine]])
    cosine, sine = turn(member_order(SECOND_TURN), np.arange(128), 128)
    inverse = np.block([[cosine, -sine], [sine, cosine]]) / NT
    return halves(forward), halves(inverse)


def inner_tables():
    cosine, sine = turn(np.arange(BLOCK), np.arange(BLOCK), BLOCK)
    eye = np.eye(4)
    cos4, sin4 = np.kron(eye, cosine), np.kron(eye, sine)
    forward = np.block([[cos4, -sin4], [sin4, cos4]])
    order = np.arange(128).reshape(4, 2, HALF).transpose(1, 0, 2).reshape(-1)
    cos4, sin4 = cos4[:, order], sin4[:, order]
    inverse = np.block([[cos4, sin4], [-sin4, cos4]])
    return halves(forward), halves(inverse)


def twist_tables():
    time = np.tile(np.arange(BLOCK), 4)
    order = np.arange(128).reshape(4, 2, HALF).transpose(1, 0, 2).reshape(-1)
    cosine, sine = turn(np.arange(128), time, NT)
    forward = np.stack([cosine, -sine])
    inverse = np.stack([cosine[:, order], sine[:, order]])
    return np.concatenate([forward, inverse]).astype(np.float32)


def split(value):
    high = value.astype(BF16)
    return high, (value - high.astype(F32)).astype(BF16)


def product(left, right, contract):
    dims = (contract, ((), ()))

    def dot(a, b):
        return lax.dot_general(a, b, dims, preferred_element_type=F32)

    return dot(left[0], right[0]) + (dot(left[0], right[1]) + dot(left[1], right[0]))


ROWS_COLS = ((1,), (0,))
ROWS_ROWS = ((1,), (1,))
COLS_COLS = ((0,), (0,))


def zonal_kernel(
    sym_hbm, wind_hbm, table_hbm, out_ref, sign_ref, sym_ref, wind_ref, table_ref, arrived
):
    cuts = (pl.ds(0, 256), pl.ds(256, NLON - 256))
    flags = pltpu.make_async_copy(sym_hbm, sym_ref, arrived.at[0])
    flags.start()
    loads = []
    for i, cut in enumerate(cuts):
        pair = [
            pltpu.make_async_copy(
                source.at[:, :, cut], target.at[:, :, cut], arrived.at[1 + 2 * i + n]
            )
            for n, (source, target) in enumerate(((wind_hbm, wind_ref), (table_hbm, table_ref)))
        ]
        for load in pair:
            load.start()
        loads.append(pair)
    flags.wait()
    signs = [1.0 - 2.0 * sym_ref[j].astype(F32) for j in range(NPAIR)]
    for j in range(NPAIR):
        sign_ref[pl.ds(j, 1), :] = jnp.full((1, NLON), signs[j], F32)
    terms = []
    for cut, pair in zip(cuts, loads):
        for load in pair:
            load.wait()
        component = jnp.concatenate(
            [
                0.5 * (wind_ref[CENTRE + j, :, cut] + signs[j] * wind_ref[CENTRE - j, :, cut])
                for j in range(NPAIR)
            ],
            axis=0,
        )
        table = (table_ref[0, :, cut], table_ref[1, :, cut])
        terms.append(product(table, split(component), ROWS_ROWS))
    coef = terms[0] + terms[1]
    for c in range(2):
        for jq in range(4):
            tile = coef[c * 128 : (c + 1) * 128, jq * 128 : (jq + 1) * 128]
            out_ref[pl.ds(c * 4 + jq, 128, stride=8), :] = tile


def time_kernel(
    series_ref, mask_ref, spread_ref, outer_f, inner_f, inner_i, outer_i, twist_ref, out_ref
):
    def rows(ref):
        return ref[0], ref[1]

    def tile(value, c, q):
        return value[c * 128 : (c + 1) * 128, q * 128 : (q + 1) * 128]

    def square(tiles):
        return jnp.concatenate([jnp.concatenate(row, axis=1) for row in tiles], axis=0)

    def partial_dft(jh):
        blocks = [
            [series_ref[pl.ds(c * 4 + jh * 2 + q, 128, stride=8), :] for q in range(2)]
            for c in range(2)
        ]
        return product(rows(outer_f), split(square(blocks)), ROWS_COLS)

    def twist(value):
        turned = []
        for q in range(2):
            real, imag = tile(value, 0, q), tile(value, 1, q)
            turned.append(
                [
                    real * twist_ref[0] - imag * twist_ref[1],
                    real * twist_ref[1] + imag * twist_ref[0],
                ]
            )
        return square(turned)

    low_lanes = lax.broadcasted_iota(jnp.int32, (128, 128), 1) < 64

    def untwist(value):
        turned = [[], []]
        for q in range(2):
            real, imag = tile(value, q, 0), tile(value, q, 1)
            turned[0].append(real * twist_ref[2] - imag * twist_ref[3])
            turned[1].append(real * twist_ref[3] + imag * twist_ref[2])
        return square(
            [
                [
                    jnp.where(low_lanes, first, pltpu.roll(second, 64, 1)),
                    jnp.where(low_lanes, pltpu.roll(first, 64, 1), second),
                ]
                for first, second in turned
            ]
        )

    partial = [partial_dft(jh) for jh in range(2)]
    twisted = [twist(value) for value in partial]
    keeps = []
    for b in range(2):
        keep = lax.dot_general(
            mask_ref[b].astype(F32).astype(BF16),
            spread_ref[...],
            (COLS_COLS, ((), ())),
            preferred_element_type=F32,
        ).astype(BF16)
        keeps.append(square([[keep, keep], [keep, keep]]))
    spectrum = [split(product(split(value), rows(inner_f), ROWS_COLS)) for value in twisted]
    parts = [(b, jh) for b in range(2) for jh in range(2)]
    unwound = [
        product((spectrum[jh][0] * keeps[b], spectrum[jh][1] * keeps[b]), rows(inner_i), ROWS_COLS)
        for b, jh in parts
    ]
    untwisted = [untwist(value) for value in unwound]
    final = [product(rows(outer_i), split(value), ROWS_COLS) for value in untwisted]
    for (b, jh), restored in zip(parts, final):
        for th in range(2):
            for c in range(2):
                row = ((b * 2 + th) * 2 + c) * 2 + jh
                out_ref[pl.ds(row, 128, stride=16), :] = tile(restored, c, th)


def write_rows(out_ref, waves, sign_ref):
    for j in range(NPAIR):
        block = waves[j * HALF : (j + 1) * HALF, :]
        out_ref[CENTRE + j] = block
        if j:
            out_ref[CENTRE - j] = sign_ref[pl.ds(j, 1), :] * block


def waves_kernel(sign_ref, coef_ref, table_ref, kelvin_ref, mjo_ref):
    th = pl.program_id(0)
    table = (table_ref[0], table_ref[1])
    for b, out_ref in ((0, kelvin_ref), (1, mjo_ref)):
        row = (b * 2 + th) * 4
        coef = jnp.concatenate(
            [
                jnp.concatenate(
                    [coef_ref[pl.ds(row + c * 2 + jh, 128, stride=16), :] for jh in range(2)],
                    axis=1,
                )
                for c in range(2)
            ],
            axis=0,
        )
        write_rows(out_ref, product(split(coef), table, COLS_COLS), sign_ref)


def pick_kernel(coef_ref, *out_refs):
    first = 8 + (1 - lax.axis_index("lv")) * 4
    for jh, out_ref in enumerate(out_refs):
        for c in range(2):
            out_ref[pl.ds(c * 128, 128), :] = coef_ref[pl.ds(first + c * 2 + jh, 128, stride=16), :]


def shear_kernel(jh, sign_ref, coef_ref, partner_ref, table_ref, *rest):
    out_hbm, rows_ref, sent = rest[-3:]
    level = lax.axis_index("lv")
    level_sign = jnp.where(level == 1, 1.0, -1.0)
    own = jnp.concatenate(
        [coef_ref[pl.ds(8 + level * 4 + c * 2 + jh, 128, stride=16), :] for c in range(2)], axis=0
    )
    apart = level_sign * (own - partner_ref[...])
    waves = product(split(apart), (table_ref[0], table_ref[1]), COLS_COLS)
    centre = (7, 15)[jh]
    blocks = [waves[i * HALF : (i + 1) * HALF, :] for i in range(8)]
    stores = []

    def send(source, target, count):
        stores.append(
            pltpu.make_async_copy(
                rows_ref.at[pl.ds(source, count)],
                out_hbm.at[pl.ds(target, count)],
                sent.at[len(stores)],
            )
        )
        stores[-1].start()

    for i, block in enumerate(blocks):
        rows_ref[7 + i + jh] = block
    if jh:
        send(8, 23, 8)
    for i, block in enumerate(blocks):
        j = jh * 8 + i
        if j:
            rows_ref[centre - j] = sign_ref[pl.ds(j, 1), :] * block
    send(0, 8 * (1 - jh), 15 - 7 * jh)
    for store in stores:
        store.wait()


VMEM = pl.BlockSpec(memory_space=pltpu.VMEM)
HBM = pl.BlockSpec(memory_space=pltpu.HBM)


def call(kernel, in_specs, out_shapes, macs, moved, **kwargs):
    return pl.pallas_call(
        kernel,
        in_specs=in_specs,
        out_shape=out_shapes,
        cost_estimate=pl.CostEstimate(flops=2 * macs, bytes_accessed=moved, transcendentals=0),
        compiler_params=pltpu.CompilerParams(vmem_limit_bytes=32 << 20),
        **kwargs,
    )


def in_hbm(array):
    return pltpu.with_memory_space_constraint(array, pltpu.HBM)


def shape(*sizes):
    return jax.ShapeDtypeStruct(sizes, F32)


def body(wind_field, band_mask, sym_flag):
    record = jnp.transpose(wind_field[0], (1, 0, 2))
    outer_f, outer_i = outer_tables()
    inner_f, inner_i = inner_tables()
    spread = np.tile(np.eye(BLOCK), (1, 4)).astype(ml_dtypes.bfloat16)
    inverse_table = zonal_inverse_table()

    coef, signs = call(
        zonal_kernel,
        [HBM] * 3,
        (shape(1024, 128), shape(NPAIR, NLON)),
        3 * 512 * 360 * 256,
        3 << 20,
        out_specs=(VMEM, VMEM),
        scratch_shapes=[
            pltpu.SMEM((NPAIR,), jnp.int32),
            pltpu.VMEM((NLAT, BLOCK, NLON), F32),
            pltpu.VMEM((2, 2 * KM, NLON), BF16),
            pltpu.SemaphoreType.DMA((5,)),
        ],
    )(in_hbm(sym_flag), in_hbm(record), in_hbm(jnp.asarray(zonal_forward_table())))
    series = exchange(coef, FIRST_TURN)
    filtered = call(
        time_kernel, [VMEM] * 8, shape(2048, 128), 3 * 4 * 512 * 256 * 256, 4 << 20, out_specs=VMEM
    )(
        series,
        band_mask.reshape(2, BLOCK, 128),
        spread,
        outer_f,
        inner_f,
        inner_i,
        outer_i,
        twist_tables(),
    )
    returned = exchange(filtered, SECOND_TURN)
    picked = call(
        pick_kernel, [VMEM], (shape(256, 128),) * 2, 1 << 10, 1 << 20, out_specs=(VMEM,) * 2
    )(returned)
    partner = [lax.ppermute(other, "lv", [(0, 1), (1, 0)]) for other in picked]
    block = pl.BlockSpec((NLAT, HALF, NLON), lambda i: (0, i, 0))
    kelvin, mjo = call(
        waves_kernel,
        [VMEM, VMEM, VMEM],
        (shape(NLAT, BLOCK, NLON), shape(NLAT, BLOCK, NLON)),
        3 * 1024 * 360 * 256,
        5 << 20,
        grid=(2,),
        out_specs=(block, block),
    )(signs, returned, inverse_table)
    shear = []
    for jh in range(2):
        shear = [
            call(
                functools.partial(shear_kernel, jh),
                [VMEM] * 4 + [HBM] * jh,
                shape(NLAT, HALF, NLON),
                3 * 128 * 360 * 256,
                1 << 20,
                out_specs=HBM,
                scratch_shapes=[
                    pltpu.VMEM((16, HALF, NLON), F32),
                    pltpu.SemaphoreType.DMA((2,)),
                ],
                input_output_aliases={4: 0} if jh else {},
            )(signs, returned, partner[jh], inverse_table, *shear)
        ]
    return (
        jnp.transpose(kelvin, (1, 0, 2))[None],
        jnp.transpose(mjo, (1, 0, 2))[None],
        jnp.transpose(shear[0], (1, 0, 2)),
    )


def solution(mesh):
    placed = (P("lv", "ta", None, None), P(None, "ta", None), P())
    return jax.shard_map(
        body,
        mesh=mesh,
        in_specs=placed,
        out_specs=(
            P("lv", "ta", None, None),
            P("lv", "ta", None, None),
            P(("ta", "lv"), None, None),
        ),
        check_vma=False,
    )
```

```python
import functools

import jax
import jax.numpy as jnp
import ml_dtypes
import numpy as np
from jax import lax
from jax.experimental import pallas as pl
from jax.experimental.pallas import tpu as pltpu
from jax.sharding import PartitionSpec as P

NLON = 360
NLAT = 31
KM = 128
NT = 4096
NPAIR = 16
BLOCK = 32
HALF = 16
CENTRE = NPAIR - 1
FIRST_TURN = (2, 1, 4, 1)
SECOND_TURN = (2, 1, 4, 1)
F32 = jnp.float32
BF16 = jnp.bfloat16


def member_order(turn_by):
    index = np.arange(128).reshape(4, 2, 8, 2)
    return np.roll(index, turn_by, axis=(0, 1, 2, 3)).reshape(-1)


def exchange(blocks, turn_by):
    groups = [[int(member) for member in member_order(turn_by)]]
    return lax.all_to_all(
        blocks, "ta", split_axis=0, concat_axis=0, axis_index_groups=groups, tiled=True
    )


def halves(table):
    table = np.asarray(table, np.float32)
    high = table.astype(ml_dtypes.bfloat16)
    low = (table - high.astype(np.float32)).astype(ml_dtypes.bfloat16)
    return np.stack([high, low])


def turn(rows, cols, length):
    angle = 2.0 * np.pi / length * (np.outer(rows, cols) % length)
    return np.cos(angle), np.sin(angle)


def zonal_forward_table():
    cosine, sine = turn(member_order(FIRST_TURN), np.arange(NLON), NLON)
    return halves(np.concatenate([cosine, -sine]) / NLON * 0.5)


def zonal_inverse_table():
    wavenumber = member_order(SECOND_TURN)
    cosine, sine = turn(wavenumber, np.arange(NLON), NLON)
    doubled = np.where(wavenumber == 0, 1.0, 2.0)[:, None]
    return halves(np.concatenate([cosine * doubled, -sine * doubled]))


def outer_tables():
    cosine, sine = turn(np.arange(128), member_order(FIRST_TURN), 128)
    forward = np.block([[cosine, sine], [-sine, cosine]])
    cosine, sine = turn(member_order(SECOND_TURN), np.arange(128), 128)
    inverse = np.block([[cosine, -sine], [sine, cosine]]) / NT
    return halves(forward), halves(inverse)


def inner_tables():
    cosine, sine = turn(np.arange(BLOCK), np.arange(BLOCK), BLOCK)
    eye = np.eye(4)
    cos4, sin4 = np.kron(eye, cosine), np.kron(eye, sine)
    forward = np.block([[cos4, -sin4], [sin4, cos4]])
    order = np.arange(128).reshape(4, 2, HALF).transpose(1, 0, 2).reshape(-1)
    cos4, sin4 = cos4[:, order], sin4[:, order]
    inverse = np.block([[cos4, sin4], [-sin4, cos4]])
    return halves(forward), halves(inverse)


def twist_tables():
    time = np.tile(np.arange(BLOCK), 4)
    order = np.arange(128).reshape(4, 2, HALF).transpose(1, 0, 2).reshape(-1)
    cosine, sine = turn(np.arange(128), time, NT)
    forward = np.stack([cosine, -sine])
    inverse = np.stack([cosine[:, order], sine[:, order]])
    return np.concatenate([forward, inverse]).astype(np.float32)


def split(value):
    high = value.astype(BF16)
    return high, (value - high.astype(F32)).astype(BF16)


def product(left, right, contract):
    dims = (contract, ((), ()))

    def dot(a, b):
        return lax.dot_general(a, b, dims, preferred_element_type=F32)

    return dot(left[0], right[0]) + (dot(left[0], right[1]) + dot(left[1], right[0]))


ROWS_COLS = ((1,), (0,))
ROWS_ROWS = ((1,), (1,))
COLS_COLS = ((0,), (0,))


def zonal_kernel(
    sym_hbm, wind_hbm, table_hbm, out_ref, sign_ref, sym_ref, wind_ref, table_ref, arrived
):
    cuts = (pl.ds(0, 256), pl.ds(256, NLON - 256))
    flags = pltpu.make_async_copy(sym_hbm, sym_ref, arrived.at[0])
    flags.start()
    loads = []
    for i, cut in enumerate(cuts):
        pair = [
            pltpu.make_async_copy(
                source.at[:, :, cut], target.at[:, :, cut], arrived.at[1 + 2 * i + n]
            )
            for n, (source, target) in enumerate(((wind_hbm, wind_ref), (table_hbm, table_ref)))
        ]
        for load in pair:
            load.start()
        loads.append(pair)
    flags.wait()
    signs = [1.0 - 2.0 * sym_ref[j].astype(F32) for j in range(NPAIR)]
    for j in range(NPAIR):
        sign_ref[pl.ds(j, 1), :] = jnp.full((1, NLON), signs[j], F32)
    terms = []
    for cut, pair in zip(cuts, loads):
        for load in pair:
            load.wait()
        component = jnp.concatenate(
            [
                wind_ref[CENTRE + j, :, cut] + signs[j] * wind_ref[CENTRE - j, :, cut]
                for j in range(NPAIR)
            ],
            axis=0,
        )
        table = (table_ref[0, :, cut], table_ref[1, :, cut])
        terms.append(product(table, split(component), ROWS_ROWS))
    coef = terms[0] + terms[1]
    for c in range(2):
        for jq in range(4):
            tile = coef[c * 128 : (c + 1) * 128, jq * 128 : (jq + 1) * 128]
            out_ref[pl.ds(c * 4 + jq, 128, stride=8), :] = tile


def time_kernel(
    series_ref, mask_ref, spread_ref, outer_f, inner_f, inner_i, outer_i, twist_ref, out_ref
):
    def rows(ref):
        return ref[0], ref[1]

    def tile(value, c, q):
        return value[c * 128 : (c + 1) * 128, q * 128 : (q + 1) * 128]

    def square(tiles):
        return jnp.concatenate([jnp.concatenate(row, axis=1) for row in tiles], axis=0)

    def partial_dft(jh):
        blocks = [
            [series_ref[pl.ds(c * 4 + jh * 2 + q, 128, stride=8), :] for q in range(2)]
            for c in range(2)
        ]
        return product(rows(outer_f), split(square(blocks)), ROWS_COLS)

    def twist(value):
        turned = []
        for q in range(2):
            real, imag = tile(value, 0, q), tile(value, 1, q)
            turned.append(
                [
                    real * twist_ref[0] - imag * twist_ref[1],
                    real * twist_ref[1] + imag * twist_ref[0],
                ]
            )
        return square(turned)

    low_lanes = lax.broadcasted_iota(jnp.int32, (128, 128), 1) < 64

    def untwist(value):
        turned = [[], []]
        for q in range(2):
            real, imag = tile(value, q, 0), tile(value, q, 1)
            turned[0].append(real * twist_ref[2] - imag * twist_ref[3])
            turned[1].append(real * twist_ref[3] + imag * twist_ref[2])
        return square(
            [
                [
                    jnp.where(low_lanes, first, pltpu.roll(second, 64, 1)),
                    jnp.where(low_lanes, pltpu.roll(first, 64, 1), second),
                ]
                for first, second in turned
            ]
        )

    partial = [partial_dft(jh) for jh in range(2)]
    twisted = [twist(value) for value in partial]
    keeps = []
    for b in range(2):
        keep = lax.dot_general(
            mask_ref[b].astype(F32).astype(BF16),
            spread_ref[...],
            (COLS_COLS, ((), ())),
            preferred_element_type=F32,
        ).astype(BF16)
        keeps.append(square([[keep, keep], [keep, keep]]))
    spectrum = [split(product(split(value), rows(inner_f), ROWS_COLS)) for value in twisted]
    parts = [(b, jh) for b in range(2) for jh in range(2)]
    unwound = [
        product((spectrum[jh][0] * keeps[b], spectrum[jh][1] * keeps[b]), rows(inner_i), ROWS_COLS)
        for b, jh in parts
    ]
    untwisted = [untwist(value) for value in unwound]
    final = [product(rows(outer_i), split(value), ROWS_COLS) for value in untwisted]
    for (b, jh), restored in zip(parts, final):
        for th in range(2):
            for c in range(2):
                row = ((b * 2 + th) * 2 + c) * 2 + jh
                out_ref[pl.ds(row, 128, stride=16), :] = tile(restored, c, th)


def write_rows(out_ref, waves, sign_ref):
    for j in range(NPAIR):
        block = waves[j * HALF : (j + 1) * HALF, :]
        out_ref[CENTRE + j] = block
        if j:
            out_ref[CENTRE - j] = sign_ref[pl.ds(j, 1), :] * block


def waves_kernel(sign_ref, coef_ref, table_ref, kelvin_ref, mjo_ref):
    th = pl.program_id(0)
    table = (table_ref[0], table_ref[1])
    for b, out_ref in ((0, kelvin_ref), (1, mjo_ref)):
        row = (b * 2 + th) * 4
        coef = jnp.concatenate(
            [
                jnp.concatenate(
                    [coef_ref[pl.ds(row + c * 2 + jh, 128, stride=16), :] for jh in range(2)],
                    axis=1,
                )
                for c in range(2)
            ],
            axis=0,
        )
        write_rows(out_ref, product(split(coef), table, COLS_COLS), sign_ref)


def pick_kernel(coef_ref, *out_refs):
    first = 8 + (1 - lax.axis_index("lv")) * 4
    for jh, out_ref in enumerate(out_refs):
        for c in range(2):
            out_ref[pl.ds(c * 128, 128), :] = coef_ref[pl.ds(first + c * 2 + jh, 128, stride=16), :]


def shear_kernel(jh, sign_ref, coef_ref, partner_ref, table_ref, *rest):
    out_hbm, rows_ref, sent = rest[-3:]
    level = lax.axis_index("lv")
    level_sign = jnp.where(level == 1, 1.0, -1.0)
    own = jnp.concatenate(
        [coef_ref[pl.ds(8 + level * 4 + c * 2 + jh, 128, stride=16), :] for c in range(2)], axis=0
    )
    apart = level_sign * (own - partner_ref[...])
    waves = product(split(apart), (table_ref[0], table_ref[1]), COLS_COLS)
    centre = (7, 15)[jh]
    blocks = [waves[i * HALF : (i + 1) * HALF, :] for i in range(8)]
    stores = []

    def send(source, target, count):
        stores.append(
            pltpu.make_async_copy(
                rows_ref.at[pl.ds(source, count)],
                out_hbm.at[pl.ds(target, count)],
                sent.at[len(stores)],
            )
        )
        stores[-1].start()

    for i, block in enumerate(blocks):
        rows_ref[7 + i + jh] = block
    if jh:
        send(8, 23, 8)
    for i, block in enumerate(blocks):
        j = jh * 8 + i
        if j:
            rows_ref[centre - j] = sign_ref[pl.ds(j, 1), :] * block
    send(0, 8 * (1 - jh), 15 - 7 * jh)
    for store in stores:
        store.wait()


VMEM = pl.BlockSpec(memory_space=pltpu.VMEM)
HBM = pl.BlockSpec(memory_space=pltpu.HBM)


def call(kernel, in_specs, out_shapes, macs, moved, **kwargs):
    return pl.pallas_call(
        kernel,
        in_specs=in_specs,
        out_shape=out_shapes,
        cost_estimate=pl.CostEstimate(flops=2 * macs, bytes_accessed=moved, transcendentals=0),
        compiler_params=pltpu.CompilerParams(vmem_limit_bytes=32 << 20),
        **kwargs,
    )


def in_hbm(array):
    return pltpu.with_memory_space_constraint(array, pltpu.HBM)


def shape(*sizes):
    return jax.ShapeDtypeStruct(sizes, F32)


def body(wind_field, band_mask, sym_flag):
    record = jnp.transpose(wind_field[0], (1, 0, 2))
    outer_f, outer_i = outer_tables()
    inner_f, inner_i = inner_tables()
    spread = np.tile(np.eye(BLOCK), (1, 4)).astype(ml_dtypes.bfloat16)
    inverse_table = zonal_inverse_table()

    coef, signs = call(
        zonal_kernel,
        [HBM] * 3,
        (shape(1024, 128), shape(NPAIR, NLON)),
        3 * 512 * 360 * 256,
        3 << 20,
        out_specs=(VMEM, VMEM),
        scratch_shapes=[
            pltpu.SMEM((NPAIR,), jnp.int32),
            pltpu.VMEM((NLAT, BLOCK, NLON), F32),
            pltpu.VMEM((2, 2 * KM, NLON), BF16),
            pltpu.SemaphoreType.DMA((5,)),
        ],
    )(in_hbm(sym_flag), in_hbm(record), in_hbm(jnp.asarray(zonal_forward_table())))
    series = exchange(coef, FIRST_TURN)
    filtered = call(
        time_kernel, [VMEM] * 8, shape(2048, 128), 3 * 4 * 512 * 256 * 256, 4 << 20, out_specs=VMEM
    )(
        series,
        band_mask.reshape(2, BLOCK, 128),
        spread,
        outer_f,
        inner_f,
        inner_i,
        outer_i,
        twist_tables(),
    )
    returned = exchange(filtered, SECOND_TURN)
    picked = call(
        pick_kernel, [VMEM], (shape(256, 128),) * 2, 1 << 10, 1 << 20, out_specs=(VMEM,) * 2
    )(returned)
    partner = [lax.ppermute(other, "lv", [(0, 1), (1, 0)]) for other in picked]
    block = pl.BlockSpec((NLAT, HALF, NLON), lambda i: (0, i, 0))
    kelvin, mjo = call(
        waves_kernel,
        [VMEM, VMEM, VMEM],
        (shape(NLAT, BLOCK, NLON), shape(NLAT, BLOCK, NLON)),
        3 * 1024 * 360 * 256,
        5 << 20,
        grid=(2,),
        out_specs=(block, block),
    )(signs, returned, inverse_table)
    shear = []
    for jh in range(2):
        shear = [
            call(
                functools.partial(shear_kernel, jh),
                [VMEM] * 4 + [HBM] * jh,
                shape(NLAT, HALF, NLON),
                3 * 128 * 360 * 256,
                1 << 20,
                out_specs=HBM,
                scratch_shapes=[
                    pltpu.VMEM((16, HALF, NLON), F32),
                    pltpu.SemaphoreType.DMA((2,)),
                ],
                input_output_aliases={4: 0} if jh else {},
            )(signs, returned, partner[jh], inverse_table, *shear)
        ]
    return (
        jnp.transpose(kelvin, (1, 0, 2))[None],
        jnp.transpose(mjo, (1, 0, 2))[None],
        jnp.transpose(shear[0], (1, 0, 2)),
    )


def solution(mesh):
    placed = (P("lv", "ta", None, None), P(None, "ta", None), P())
    return jax.shard_map(
        body,
        mesh=mesh,
        in_specs=placed,
        out_specs=(
            P("lv", "ta", None, None),
            P("lv", "ta", None, None),
            P(("ta", "lv"), None, None),
        ),
        check_vma=False,
    )
```

```python
import functools

import jax
import jax.numpy as jnp
import ml_dtypes
import numpy as np
from jax import lax
from jax.experimental import pallas as pl
from jax.experimental.pallas import tpu as pltpu
from jax.sharding import PartitionSpec as P

NLON = 360
NLAT = 31
KM = 128
NT = 4096
NPAIR = 16
BLOCK = 32
HALF = 16
CENTRE = NPAIR - 1
FIRST_TURN = (2, 1, 4, 1)
SECOND_TURN = (2, 1, 4, 1)
F32 = jnp.float32
BF16 = jnp.bfloat16


def member_order(turn_by):
    index = np.arange(128).reshape(4, 2, 8, 2)
    return np.roll(index, turn_by, axis=(0, 1, 2, 3)).reshape(-1)


def exchange(blocks, turn_by):
    groups = [[int(member) for member in member_order(turn_by)]]
    return lax.all_to_all(
        blocks, "ta", split_axis=0, concat_axis=0, axis_index_groups=groups, tiled=True
    )


def halves(table):
    table = np.asarray(table, np.float32)
    high = table.astype(ml_dtypes.bfloat16)
    low = (table - high.astype(np.float32)).astype(ml_dtypes.bfloat16)
    return np.stack([high, low])


def turn(rows, cols, length):
    angle = 2.0 * np.pi / length * (np.outer(rows, cols) % length)
    return np.cos(angle), np.sin(angle)


def zonal_forward_table():
    cosine, sine = turn(member_order(FIRST_TURN), np.arange(NLON), NLON)
    return halves(np.concatenate([cosine, -sine]) / NLON * 0.5)


def zonal_inverse_table():
    wavenumber = member_order(SECOND_TURN)
    cosine, sine = turn(wavenumber, np.arange(NLON), NLON)
    doubled = np.where(wavenumber == 0, 1.0, 2.0)[:, None]
    return halves(np.concatenate([cosine * doubled, -sine * doubled]))


def outer_tables():
    cosine, sine = turn(np.arange(128), member_order(FIRST_TURN), 128)
    forward = np.block([[cosine, sine], [-sine, cosine]])
    cosine, sine = turn(member_order(SECOND_TURN), np.arange(128), 128)
    inverse = np.block([[cosine, -sine], [sine, cosine]]) / NT
    return halves(forward), halves(inverse)


def inner_tables():
    cosine, sine = turn(np.arange(BLOCK), np.arange(BLOCK), BLOCK)
    eye = np.eye(4)
    cos4, sin4 = np.kron(eye, cosine), np.kron(eye, sine)
    forward = np.block([[cos4, -sin4], [sin4, cos4]])
    order = np.arange(128).reshape(4, 2, HALF).transpose(1, 0, 2).reshape(-1)
    cos4, sin4 = cos4[:, order], sin4[:, order]
    inverse = np.block([[cos4, sin4], [-sin4, cos4]])
    return halves(forward), halves(inverse)


def twist_tables():
    time = np.tile(np.arange(BLOCK), 4)
    order = np.arange(128).reshape(4, 2, HALF).transpose(1, 0, 2).reshape(-1)
    cosine, sine = turn(np.arange(128), time, NT)
    forward = np.stack([cosine, -sine])
    inverse = np.stack([cosine[:, order], sine[:, order]])
    return np.concatenate([forward, inverse]).astype(np.float32)


def split(value):
    high = value.astype(BF16)
    return high, (value - high.astype(F32)).astype(BF16)


def product(left, right, contract):
    dims = (contract, ((), ()))

    def dot(a, b):
        return lax.dot_general(a, b, dims, preferred_element_type=F32)

    return dot(left[0], right[0]) + (dot(left[0], right[1]) + dot(left[1], right[0]))


ROWS_COLS = ((1,), (0,))
ROWS_ROWS = ((1,), (1,))
COLS_COLS = ((0,), (0,))


def zonal_kernel(
    sym_hbm, wind_hbm, table_hbm, out_ref, sign_ref, sym_ref, wind_ref, table_ref, arrived
):
    cuts = (pl.ds(0, 256), pl.ds(256, NLON - 256))
    flags = pltpu.make_async_copy(sym_hbm, sym_ref, arrived.at[0])
    flags.start()
    loads = []
    for i, cut in enumerate(cuts):
        pair = [
            pltpu.make_async_copy(
                source.at[:, :, cut], target.at[:, :, cut], arrived.at[1 + 2 * i + n]
            )
            for n, (source, target) in enumerate(((table_hbm, table_ref), (wind_hbm, wind_ref)))
        ]
        for load in pair:
            load.start()
        loads.append(pair)
    flags.wait()
    signs = [1.0 - 2.0 * sym_ref[j].astype(F32) for j in range(NPAIR)]
    for j in range(NPAIR):
        sign_ref[pl.ds(j, 1), :] = jnp.full((1, NLON), signs[j], F32)
    terms = []
    for cut, pair in zip(cuts, loads):
        for load in pair:
            load.wait()
        component = jnp.concatenate(
            [
                wind_ref[CENTRE + j, :, cut] + signs[j] * wind_ref[CENTRE - j, :, cut]
                for j in range(NPAIR)
            ],
            axis=0,
        )
        table = (table_ref[0, :, cut], table_ref[1, :, cut])
        terms.append(product(table, split(component), ROWS_ROWS))
    coef = terms[0] + terms[1]
    for c in range(2):
        for jq in range(4):
            tile = coef[c * 128 : (c + 1) * 128, jq * 128 : (jq + 1) * 128]
            out_ref[pl.ds(c * 4 + jq, 128, stride=8), :] = tile


def time_kernel(
    series_ref, mask_ref, spread_ref, outer_f, inner_f, inner_i, outer_i, twist_ref, out_ref
):
    def rows(ref):
        return ref[0], ref[1]

    def tile(value, c, q):
        return value[c * 128 : (c + 1) * 128, q * 128 : (q + 1) * 128]

    def square(tiles):
        return jnp.concatenate([jnp.concatenate(row, axis=1) for row in tiles], axis=0)

    def partial_dft(jh):
        blocks = [
            [series_ref[pl.ds(c * 4 + jh * 2 + q, 128, stride=8), :] for q in range(2)]
            for c in range(2)
        ]
        return product(rows(outer_f), split(square(blocks)), ROWS_COLS)

    def twist(value):
        turned = []
        for q in range(2):
            real, imag = tile(value, 0, q), tile(value, 1, q)
            turned.append(
                [
                    real * twist_ref[0] - imag * twist_ref[1],
                    real * twist_ref[1] + imag * twist_ref[0],
                ]
            )
        return square(turned)

    low_lanes = lax.broadcasted_iota(jnp.int32, (128, 128), 1) < 64

    def untwist(value):
        turned = [[], []]
        for q in range(2):
            real, imag = tile(value, q, 0), tile(value, q, 1)
            turned[0].append(real * twist_ref[2] - imag * twist_ref[3])
            turned[1].append(real * twist_ref[3] + imag * twist_ref[2])
        return square(
            [
                [
                    jnp.where(low_lanes, first, pltpu.roll(second, 64, 1)),
                    jnp.where(low_lanes, pltpu.roll(first, 64, 1), second),
                ]
                for first, second in turned
            ]
        )

    partial = [partial_dft(jh) for jh in range(2)]
    twisted = [twist(value) for value in partial]
    keeps = []
    for b in range(2):
        keep = lax.dot_general(
            mask_ref[b].astype(F32).astype(BF16),
            spread_ref[...],
            (COLS_COLS, ((), ())),
            preferred_element_type=F32,
        ).astype(BF16)
        keeps.append(square([[keep, keep], [keep, keep]]))
    spectrum = [split(product(split(value), rows(inner_f), ROWS_COLS)) for value in twisted]
    parts = [(b, jh) for b in range(2) for jh in range(2)]
    unwound = [
        product((spectrum[jh][0] * keeps[b], spectrum[jh][1] * keeps[b]), rows(inner_i), ROWS_COLS)
        for b, jh in parts
    ]
    untwisted = [untwist(value) for value in unwound]
    final = [product(rows(outer_i), split(value), ROWS_COLS) for value in untwisted]
    for (b, jh), restored in zip(parts, final):
        for th in range(2):
            for c in range(2):
                row = ((b * 2 + th) * 2 + c) * 2 + jh
                out_ref[pl.ds(row, 128, stride=16), :] = tile(restored, c, th)


def write_rows(out_ref, waves, sign_ref):
    for j in range(NPAIR):
        block = waves[j * HALF : (j + 1) * HALF, :]
        out_ref[CENTRE + j] = block
        if j:
            out_ref[CENTRE - j] = sign_ref[pl.ds(j, 1), :] * block


def waves_kernel(sign_ref, coef_ref, table_ref, kelvin_ref, mjo_ref):
    th = pl.program_id(0)
    table = (table_ref[0], table_ref[1])
    for b, out_ref in ((0, kelvin_ref), (1, mjo_ref)):
        row = (b * 2 + th) * 4
        coef = jnp.concatenate(
            [
                jnp.concatenate(
                    [coef_ref[pl.ds(row + c * 2 + jh, 128, stride=16), :] for jh in range(2)],
                    axis=1,
                )
                for c in range(2)
            ],
            axis=0,
        )
        write_rows(out_ref, product(split(coef), table, COLS_COLS), sign_ref)


def pick_kernel(coef_ref, *out_refs):
    first = 8 + (1 - lax.axis_index("lv")) * 4
    for jh, out_ref in enumerate(out_refs):
        for c in range(2):
            out_ref[pl.ds(c * 128, 128), :] = coef_ref[pl.ds(first + c * 2 + jh, 128, stride=16), :]


def shear_kernel(jh, sign_ref, coef_ref, partner_ref, table_ref, *rest):
    out_hbm, rows_ref, sent = rest[-3:]
    level = lax.axis_index("lv")
    level_sign = jnp.where(level == 1, 1.0, -1.0)
    own = jnp.concatenate(
        [coef_ref[pl.ds(8 + level * 4 + c * 2 + jh, 128, stride=16), :] for c in range(2)], axis=0
    )
    apart = level_sign * (own - partner_ref[...])
    waves = product(split(apart), (table_ref[0], table_ref[1]), COLS_COLS)
    centre = (7, 15)[jh]
    blocks = [waves[i * HALF : (i + 1) * HALF, :] for i in range(8)]
    stores = []

    def send(source, target, count):
        stores.append(
            pltpu.make_async_copy(
                rows_ref.at[pl.ds(source, count)],
                out_hbm.at[pl.ds(target, count)],
                sent.at[len(stores)],
            )
        )
        stores[-1].start()

    for i, block in enumerate(blocks):
        rows_ref[7 + i + jh] = block
    if jh:
        send(8, 23, 8)
    for i, block in enumerate(blocks):
        j = jh * 8 + i
        if j:
            rows_ref[centre - j] = sign_ref[pl.ds(j, 1), :] * block
    send(0, 8 * (1 - jh), 15 - 7 * jh)
    for store in stores:
        store.wait()


VMEM = pl.BlockSpec(memory_space=pltpu.VMEM)
HBM = pl.BlockSpec(memory_space=pltpu.HBM)


def call(kernel, in_specs, out_shapes, macs, moved, **kwargs):
    return pl.pallas_call(
        kernel,
        in_specs=in_specs,
        out_shape=out_shapes,
        cost_estimate=pl.CostEstimate(flops=2 * macs, bytes_accessed=moved, transcendentals=0),
        compiler_params=pltpu.CompilerParams(vmem_limit_bytes=32 << 20),
        **kwargs,
    )


def in_hbm(array):
    return pltpu.with_memory_space_constraint(array, pltpu.HBM)


def shape(*sizes):
    return jax.ShapeDtypeStruct(sizes, F32)


def body(wind_field, band_mask, sym_flag):
    record = jnp.transpose(wind_field[0], (1, 0, 2))
    outer_f, outer_i = outer_tables()
    inner_f, inner_i = inner_tables()
    spread = np.tile(np.eye(BLOCK), (1, 4)).astype(ml_dtypes.bfloat16)
    inverse_table = zonal_inverse_table()

    coef, signs = call(
        zonal_kernel,
        [HBM] * 3,
        (shape(1024, 128), shape(NPAIR, NLON)),
        3 * 512 * 360 * 256,
        3 << 20,
        out_specs=(VMEM, VMEM),
        scratch_shapes=[
            pltpu.SMEM((NPAIR,), jnp.int32),
            pltpu.VMEM((NLAT, BLOCK, NLON), F32),
            pltpu.VMEM((2, 2 * KM, NLON), BF16),
            pltpu.SemaphoreType.DMA((5,)),
        ],
    )(in_hbm(sym_flag), in_hbm(record), in_hbm(jnp.asarray(zonal_forward_table())))
    series = exchange(coef, FIRST_TURN)
    filtered = call(
        time_kernel, [VMEM] * 8, shape(2048, 128), 3 * 4 * 512 * 256 * 256, 4 << 20, out_specs=VMEM
    )(
        series,
        band_mask.reshape(2, BLOCK, 128),
        spread,
        outer_f,
        inner_f,
        inner_i,
        outer_i,
        twist_tables(),
    )
    returned = exchange(filtered, SECOND_TURN)
    picked = call(
        pick_kernel, [VMEM], (shape(256, 128),) * 2, 1 << 10, 1 << 20, out_specs=(VMEM,) * 2
    )(returned)
    partner = [lax.ppermute(other, "lv", [(0, 1), (1, 0)]) for other in picked]
    block = pl.BlockSpec((NLAT, HALF, NLON), lambda i: (0, i, 0))
    kelvin, mjo = call(
        waves_kernel,
        [VMEM, VMEM, VMEM],
        (shape(NLAT, BLOCK, NLON), shape(NLAT, BLOCK, NLON)),
        3 * 1024 * 360 * 256,
        5 << 20,
        grid=(2,),
        out_specs=(block, block),
    )(signs, returned, inverse_table)
    shear = []
    for jh in range(2):
        shear = [
            call(
                functools.partial(shear_kernel, jh),
                [VMEM] * 4 + [HBM] * jh,
                shape(NLAT, HALF, NLON),
                3 * 128 * 360 * 256,
                1 << 20,
                out_specs=HBM,
                scratch_shapes=[
                    pltpu.VMEM((16, HALF, NLON), F32),
                    pltpu.SemaphoreType.DMA((2,)),
                ],
                input_output_aliases={4: 0} if jh else {},
            )(signs, returned, partner[jh], inverse_table, *shear)
        ]
    return (
        jnp.transpose(kelvin, (1, 0, 2))[None],
        jnp.transpose(mjo, (1, 0, 2))[None],
        jnp.transpose(shear[0], (1, 0, 2)),
    )


def solution(mesh):
    placed = (P("lv", "ta", None, None), P(None, "ta", None), P())
    return jax.shard_map(
        body,
        mesh=mesh,
        in_specs=placed,
        out_specs=(
            P("lv", "ta", None, None),
            P("lv", "ta", None, None),
            P(("ta", "lv"), None, None),
        ),
        check_vma=False,
    )
```
